32 devices in a mesh: dp: 16 (over z, x, core), tensor: 2 (over y).
Axes of the slice: x: 2, y: 2, z: 4, core: 2. Of those that a mesh axis runs over, the one named last changes fastest.
Arguments:
- tokens: bfloat16 [6144, 1024], P('dp', 'tensor'), may hold values from -6 to 6
- cotangent: bfloat16 [6144, 1024], P('dp', 'tensor'), may hold values from -6 to 6
- attn_gain: float32 [1024], replicated, may hold values from 0.5 to 1.5
- query_weight: bfloat16 [1024, 2048], P(None, 'tensor'), may hold values from -0.1875 to 0.1875
- key_matrix: bfloat16 [1024, 1024], P(None, 'tensor'), may hold values from -0.1875 to 0.1875
- value_matrix: bfloat16 [1024, 1024], P(None, 'tensor'), may hold values from -0.1875 to 0.1875
- query_gain: float32 [128], replicated, may hold values from 1 to 2
- key_norm_gain: float32 [128], replicated, may hold values from 1 to 2
- out_weight: bfloat16 [2048, 1024], P('tensor'), may hold values from -0.75 to 0.75
- mlp_gain: float32 [1024], replicated, may hold values from 0.5 to 1.5
- gate_weight: bfloat16 [1024, 3072], P(None, 'tensor'), may hold values from -0.1875 to 0.1875
- up_weight: bfloat16 [1024, 3072], P(None, 'tensor'), may hold values from -0.1875 to 0.1875
- down_weight: bfloat16 [3072, 1024], P('tensor'), may hold values from -0.21875 to 0.21875
Outputs:
- layer_out: bfloat16 [6144, 1024], P('dp', 'tensor')
- input_grad: bfloat16 [6144, 1024], P('dp', 'tensor')
- attn_gain_grad: float32 [1024], replicated
- query_weight_grad: float32 [1024, 2048], P(None, 'tensor')
- key_weight_grad: float32 [1024, 1024], P(None, 'tensor')
- value_weight_grad: float32 [1024, 1024], P(None, 'tensor')
- query_gain_grad: float32 [128], replicated
- key_gain_grad: float32 [128], replicated
- out_weight_grad: float32 [2048, 1024], P('tensor')
- mlp_gain_grad: float32 [1024], replicated
- gate_weight_grad: float32 [1024, 3072], P(None, 'tensor')
- up_weight_grad: float32 [1024, 3072], P(None, 'tensor')
- down_weight_grad: float32 [3072, 1024], P('tensor')
The draws below stay inside these ranges and needn't reach their ends.
All inputs are finite; a program needn't handle non-finite values.
Results may differ from the reference program's by a relative error of at most 0.025.
Values may be sent and summed in bfloat16 or wider, within the bound.
No kernel may reach another device: no remote copies, remote signals or barrier semaphores. Data moves between devices by JAX's collectives and lax.ppermute only.
A program may use at most 192 MiB of HBM per device.

```python
import math
import jax
import jax.numpy as jnp
from jax import lax

MODEL_DIM = 1024
QUERY_HEADS = 16
KEY_VALUE_HEADS = 8
HEAD_SIZE = 128
FF = 3072
SEQUENCE_LENGTH = 384
BLOCK = 384
SEQS = 16
TOKENS = 6144


def block_scale(stream_key, extent, shards, low, largest):
    def one(dim, parts):
        heights = jax.random.uniform(jax.random.fold_in(jax.random.fold_in(stream_key, 6), dim), (parts,), jnp.float32, low / len(shards), largest / len(shards))
        return jnp.repeat(jnp.exp(heights), extent[dim] // parts).reshape((-1,) + (1,) * (len(extent) - dim - 1))

    factor_of = one(*shards[0])
    for cut in shards[1:]:
        factor_of = factor_of * one(*cut)
    return factor_of


def gaussian(key, shape, width, bound, cuts=(), kind=jnp.bfloat16):
    array = width * jax.random.normal(key, shape, jnp.float32)
    if cuts:
        array = array * block_scale(key, shape, cuts, -0.22, 0.18)
    return jnp.clip(array, -bound, bound).astype(kind)


def setup_inputs(seed: int = 0) -> dict:
    key_of = jax.random.split(jax.random.key(seed), 14)
    return {
        "tokens": gaussian(key_of[0], (TOKENS, MODEL_DIM), 1.0, 6.0, ((0, 16), (1, 2))),
        "cotangent": gaussian(key_of[1], (TOKENS, MODEL_DIM), 1.0, 6.0, ((0, 16), (1, 2))),
        "attn_gain": jnp.clip(1.0 + 0.1 * jax.random.normal(key_of[2], (MODEL_DIM,), jnp.float32), 0.5, 1.5),
        "query_weight": gaussian(key_of[3], (MODEL_DIM, QUERY_HEADS * HEAD_SIZE), MODEL_DIM ** -0.5, 0.1875, ((1, 2),)),
        "key_matrix": gaussian(key_of[4], (MODEL_DIM, KEY_VALUE_HEADS * HEAD_SIZE), MODEL_DIM ** -0.5, 0.1875, ((1, 2),)),
        "value_matrix": gaussian(key_of[5], (MODEL_DIM, KEY_VALUE_HEADS * HEAD_SIZE), MODEL_DIM ** -0.5, 0.1875, ((1, 2),)),
        "query_gain": jnp.clip(jax.random.uniform(key_of[6], (HEAD_SIZE,), jnp.float32, 1.0, 2.0), 1.0, 2.0),
        "key_norm_gain": jnp.clip(jax.random.uniform(key_of[7], (HEAD_SIZE,), jnp.float32, 1.0, 2.0), 1.0, 2.0),
        "out_weight": gaussian(key_of[8], (QUERY_HEADS * HEAD_SIZE, MODEL_DIM), (QUERY_HEADS * HEAD_SIZE // 32) ** -0.5, 0.75, ((0, 2),)),
        "mlp_gain": jnp.clip(1.0 + 0.1 * jax.random.normal(key_of[9], (MODEL_DIM,), jnp.float32), 0.5, 1.5),
        "gate_weight": gaussian(key_of[10], (MODEL_DIM, FF), MODEL_DIM ** -0.5, 0.1875, ((1, 2),)),
        "up_weight": gaussian(key_of[11], (MODEL_DIM, FF), MODEL_DIM ** -0.5, 0.1875, ((1, 2),)),
        "down_weight": gaussian(key_of[12], (FF, MODEL_DIM), (FF // 4) ** -0.5, 0.21875, ((0, 2),)),
    }


epsilon = 1e-06
rope_base = 1000000.0
precise = lax.Precision.HIGHEST

@jax.custom_vjp
def lowered_rows(v):
    return lax.optimization_barrier(v.astype(jnp.bfloat16)).astype(jnp.float32)

@jax.custom_vjp
def low_back(v):
    return v

def low_keep(v):
    return (lowered_rows(v), None)

def low_pass(kept, grad):
    return (grad,)

def back_keep(v):
    return (v, None)

def back_low(kept, grad):
    return (lowered_rows(grad),)
lowered_rows.defvjp(low_keep, low_pass)
low_back.defvjp(back_keep, back_low)

def norm_rows(values, gain_vec):
    return values * lax.rsqrt(lax.optimization_barrier(jnp.mean(values * values, -1, keepdims=True)) + epsilon) * gain_vec

def rotary_embed(values, token_positions):
    half_width = values.shape[-1] // 2
    steps_up = jnp.arange(half_width, dtype=jnp.float32) * (2.0 / values.shape[-1])
    frequency = rope_base ** (-steps_up)
    angle_grid = token_positions.astype(jnp.float32)[:, None] * frequency[None, :]
    cosine = jnp.cos(angle_grid)[:, None, :]
    sine_part = jnp.sin(angle_grid)[:, None, :]
    front_half = values[..., :half_width]
    back_half = values[..., half_width:]
    return jnp.concatenate([front_half * cosine - back_half * sine_part, back_half * cosine + front_half * sine_part], -1)

def matmul(left, right):
    return jnp.dot(left, right, precision=precise, preferred_element_type=jnp.float32)

def attend_heads(query_all, key_all, value_all):
    sequence_count = query_all.shape[0]

    def one_block(block_index):
        row_start = (block_index * BLOCK).astype(jnp.int32)
        query_blk = lax.dynamic_slice_in_dim(query_all, row_start, BLOCK, 1)
        scores = jnp.einsum('sqhgd,skhd->shgqk', query_blk, key_all, precision=precise)
        scores = low_back(scores)
        query_pos = row_start + jnp.arange(BLOCK, dtype=jnp.int32)
        key_pos = jnp.arange(SEQUENCE_LENGTH, dtype=jnp.int32)
        allowed = key_pos[None, :] <= query_pos[:, None]
        scores = jnp.where(allowed, scores, -1e+30)
        top_score = lax.optimization_barrier(jnp.max(scores, -1, keepdims=True))
        raised = jnp.exp(scores - top_score)
        attn_prob = lowered_rows(raised / lax.optimization_barrier(jnp.sum(raised, -1, keepdims=True)))
        return jnp.einsum('shgqk,skhd->sqhgd', attn_prob, value_all, precision=precise)
    blocks = lax.map(jax.checkpoint(one_block), jnp.arange(SEQUENCE_LENGTH // BLOCK, dtype=jnp.int32))
    blocks = jnp.moveaxis(blocks, 0, 1)
    return blocks.reshape(sequence_count, SEQUENCE_LENGTH, query_all.shape[2], query_all.shape[3], query_all.shape[4])

def group_layer(params, block_rows):
    attn_gain, query_weight, key_matrix, value_matrix, query_gain, key_norm_gain, out_weight, mlp_gain, gate_weight, up_weight, down_weight = params
    total_rows = block_rows.shape[0]
    sequence_count = total_rows // SEQUENCE_LENGTH
    heads_per_group = QUERY_HEADS // KEY_VALUE_HEADS
    score_scale = HEAD_SIZE ** (-0.5)
    normed_one = lowered_rows(norm_rows(block_rows, attn_gain))
    query_raw = low_back(matmul(normed_one, query_weight))
    key_projected = low_back(matmul(normed_one, key_matrix))
    value_lowered = lowered_rows(low_back(matmul(normed_one, value_matrix)))
    token_positions = jnp.arange(total_rows, dtype=jnp.int32) % SEQUENCE_LENGTH
    query_rotated = lowered_rows(rotary_embed(norm_rows(query_raw.reshape(total_rows, QUERY_HEADS, HEAD_SIZE), query_gain), token_positions) * score_scale)
    key_rotated = lowered_rows(rotary_embed(norm_rows(key_projected.reshape(total_rows, KEY_VALUE_HEADS, HEAD_SIZE), key_norm_gain), token_positions))
    attention_mixed = attend_heads(query_rotated.reshape(sequence_count, SEQUENCE_LENGTH, KEY_VALUE_HEADS, heads_per_group, HEAD_SIZE), key_rotated.reshape(sequence_count, SEQUENCE_LENGTH, KEY_VALUE_HEADS, HEAD_SIZE), value_lowered.reshape(sequence_count, SEQUENCE_LENGTH, KEY_VALUE_HEADS, HEAD_SIZE))
    attn_low = lowered_rows(low_back(attention_mixed.reshape(total_rows, QUERY_HEADS * HEAD_SIZE)))
    branch = low_back(matmul(attn_low, out_weight))
    middle = block_rows + branch
    normed_two = lowered_rows(norm_rows(middle, mlp_gain))
    gate_val = low_back(matmul(normed_two, gate_weight))
    up_val = low_back(matmul(normed_two, up_weight))
    hidden = lowered_rows(jax.nn.silu(gate_val) * up_val)
    return middle + low_back(matmul(hidden, down_weight))

def forward(tokens_in, params):
    group_seqs = math.gcd(SEQS, 4)
    grouped = tokens_in.reshape(SEQS // group_seqs, group_seqs * SEQUENCE_LENGTH, MODEL_DIM)

    def step_fn(unused_state, block_rows):
        return (unused_state, jax.checkpoint(group_layer)(params, block_rows))
    _, outputs = lax.scan(step_fn, jnp.zeros((), jnp.float32), grouped)
    return outputs.reshape(TOKENS, MODEL_DIM)

def reference(tokens, cotangent, attn_gain, query_weight, key_matrix, value_matrix, query_gain, key_norm_gain, out_weight, mlp_gain, gate_weight, up_weight, down_weight):
    inputs = (tokens.astype(jnp.float32), attn_gain.astype(jnp.float32), query_weight.astype(jnp.float32), key_matrix.astype(jnp.float32), value_matrix.astype(jnp.float32), query_gain.astype(jnp.float32), key_norm_gain.astype(jnp.float32), out_weight.astype(jnp.float32), mlp_gain.astype(jnp.float32), gate_weight.astype(jnp.float32), up_weight.astype(jnp.float32), down_weight.astype(jnp.float32))

    def forward_all(tokens_in, *params):
        return forward(tokens_in, params)
    layer_out, pullback = jax.vjp(forward_all, *inputs)
    gradients = pullback(cotangent.astype(jnp.float32))
    return (layer_out.astype(jnp.bfloat16), gradients[0].astype(jnp.bfloat16), gradients[1], gradients[2], gradients[3], gradients[4], gradients[5], gradients[6], gradients[7], gradients[8], gradients[9], gradients[10], gradients[11])
```

```python
import functools

import jax
import jax.numpy as jnp
import numpy as np
from jax import lax
from jax.experimental import pallas as pl
from jax.experimental.pallas import tpu as pltpu
from jax.sharding import PartitionSpec as P

HEAD_SIZE = 128
SEQUENCE_LENGTH = 384
epsilon = 1e-06
rope_base = 1000000.0
F32 = jnp.float32
BF16 = jnp.bfloat16
VMEM_BYTES = 56 * 1024 * 1024


def dot_nn(a, b):
    return lax.dot_general(a, b, (((1,), (0,)), ((), ())), preferred_element_type=F32)


def dot_nt(a, b):
    return lax.dot_general(a, b, (((1,), (1,)), ((), ())), preferred_element_type=F32)


def dot_tn(a, b):
    return lax.dot_general(a, b, (((0,), (0,)), ((), ())), preferred_element_type=F32)


def rope_tables():
    half = HEAD_SIZE // 2
    frequency = rope_base ** (-np.arange(half, dtype=np.float64) * (2.0 / HEAD_SIZE))
    angle = np.arange(SEQUENCE_LENGTH, dtype=np.float64)[:, None] * frequency[None, :]
    cosine, sine = np.cos(angle), np.sin(angle)
    return (
        np.concatenate([cosine, cosine], 1).astype(np.float32),
        np.concatenate([-sine, sine], 1).astype(np.float32),
    )


def inv_rms(v):
    return lax.rsqrt(jnp.mean(v * v, -1, keepdims=True) + epsilon)


def params(n):
    return pltpu.CompilerParams(
        dimension_semantics=("arbitrary",) * n, vmem_limit_bytes=VMEM_BYTES
    )


def whole(shape):
    return pl.BlockSpec(shape, lambda *g: (0,) * len(shape))


def attn_fwd_kernel(
    x_ref, gain_ref, wq_ref, wk_ref, wv_ref, wo_ref, qg_ref, kg_ref, cos_ref, sin_ref,
    n1_ref, qraw_ref, kraw_ref, qrot_ref, krot_ref, v_ref, p_ref, al_ref, branch_ref, blow_ref,
):
    g = pl.program_id(0)
    rows = x_ref.shape[0]
    heads = wq_ref.shape[1] // HEAD_SIZE

    @pl.when(g == 0)
    def _():
        x = x_ref[...].astype(F32)
        n1_ref[...] = (x * inv_rms(x) * gain_ref[...]).astype(BF16)
        branch_ref[...] = jnp.zeros_like(branch_ref)

    n1 = n1_ref[...]
    q_raw = dot_nn(n1, wq_ref[...])
    kv = dot_nn(n1, jnp.concatenate([wk_ref[...], wv_ref[...]], 1))
    k_raw = kv[:, :HEAD_SIZE]
    v = kv[:, HEAD_SIZE:].astype(BF16)
    qraw_ref[...] = q_raw
    kraw_ref[...] = k_raw
    v_ref[...] = v
    cosine, sine = cos_ref[...], sin_ref[...]

    def rotate(raw, gain):
        n = raw * inv_rms(raw) * gain
        return n * cosine + pltpu.roll(n, HEAD_SIZE // 2, 1) * sine

    scale = HEAD_SIZE ** (-0.5)
    k_rot = rotate(k_raw, kg_ref[...]).astype(BF16)
    krot_ref[...] = k_rot
    q_rot = jnp.concatenate(
        [
            (rotate(q_raw[:, h * HEAD_SIZE : (h + 1) * HEAD_SIZE], qg_ref[...]) * scale).astype(BF16)
            for h in range(heads)
        ],
        0,
    )
    qrot_ref[...] = q_rot[None]
    scores = dot_nt(q_rot, k_rot)
    q_pos = lax.broadcasted_iota(jnp.int32, (heads * rows, rows), 0)
    for _ in range(heads - 1):
        q_pos = jnp.where(q_pos >= rows, q_pos - rows, q_pos)
    k_pos = lax.broadcasted_iota(jnp.int32, (heads * rows, rows), 1)
    scores = jnp.where(k_pos <= q_pos, scores, -1e30)
    raised = jnp.exp(scores - jnp.max(scores, -1, keepdims=True))
    prob = (raised * (1.0 / jnp.sum(raised, -1, keepdims=True))).astype(BF16)
    p_ref[...] = prob[None]
    mixed = dot_nn(prob, v).astype(BF16)
    attn_low = jnp.concatenate([mixed[h * rows : (h + 1) * rows] for h in range(heads)], 1)
    al_ref[...] = attn_low
    branch_ref[...] += dot_nn(attn_low, wo_ref[...])

    @pl.when(g == pl.num_programs(0) - 1)
    def _():
        blow_ref[...] = branch_ref[...].astype(BF16)


def attn_fwd(x, attn_gain, wq, wk, wv, wo, q_gain, k_gain, cosine, sine):
    rows, width = x.shape
    groups = wk.shape[1] // HEAD_SIZE
    heads = wq.shape[1] // wk.shape[1]
    qw = heads * HEAD_SIZE
    col = lambda n: pl.BlockSpec((rows, n), lambda g: (0, g))
    wcol = lambda n: pl.BlockSpec((width, n), lambda g: (0, g))
    sds = jax.ShapeDtypeStruct
    return pl.pallas_call(
        attn_fwd_kernel,
        grid=(groups,),
        in_specs=[
            whole((rows, width)), whole((1, width)), wcol(qw), wcol(HEAD_SIZE), wcol(HEAD_SIZE),
            pl.BlockSpec((qw, width), lambda g: (g, 0)),
            whole((1, HEAD_SIZE)), whole((1, HEAD_SIZE)), whole((rows, HEAD_SIZE)), whole((rows, HEAD_SIZE)),
        ],
        out_specs=[
            whole((rows, width)), col(qw), col(HEAD_SIZE),
            pl.BlockSpec((1, heads * rows, HEAD_SIZE), lambda g: (g, 0, 0)),
            col(HEAD_SIZE), col(HEAD_SIZE),
            pl.BlockSpec((1, heads * rows, rows), lambda g: (g, 0, 0)),
            col(qw), whole((rows, width)), whole((rows, width)),
        ],
        out_shape=[
            sds((rows, width), BF16), sds((rows, groups * qw), F32), sds((rows, groups * HEAD_SIZE), F32),
            sds((groups, heads * rows, HEAD_SIZE), BF16),
            sds((rows, groups * HEAD_SIZE), BF16), sds((rows, groups * HEAD_SIZE), BF16),
            sds((groups, heads * rows, rows), BF16),
            sds((rows, groups * qw), BF16), sds((rows, width), F32), sds((rows, width), BF16),
        ],
        compiler_params=params(1),
        name="attention_forward",
    )(x, attn_gain, wq, wk, wv, wo, q_gain, k_gain, cosine, sine)


def mlp_kernel(
    x_ref, own_ref, other_ref, gain_ref, cot_ref, wg_ref, wu_ref, wd_ref,
    mid_ref, n2_ref, hid_ref, gg_ref, ug_ref, out_ref, ngrad_ref, acc_out, acc_n,
):
    j = pl.program_id(0)

    @pl.when(j == 0)
    def _():
        middle = x_ref[...].astype(F32) + (own_ref[...] + other_ref[...].astype(F32))
        mid_ref[...] = middle
        n2_ref[...] = (middle * inv_rms(middle) * gain_ref[...]).astype(BF16)
        acc_out[...] = jnp.zeros_like(acc_out)
        acc_n[...] = jnp.zeros_like(acc_n)

    n2 = n2_ref[...]
    wg, wu, wd = wg_ref[...], wu_ref[...], wd_ref[...]
    gate = dot_nn(n2, wg)
    up = dot_nn(n2, wu)
    sig = jax.nn.sigmoid(gate)
    silu = gate * sig
    hidden = (silu * up).astype(BF16)
    hid_ref[...] = hidden
    acc_out[...] += dot_nn(hidden, wd)
    hgrad = dot_nt(cot_ref[...], wd)
    ggrad = (hgrad * up * sig * (1.0 + gate * (1.0 - sig))).astype(BF16)
    ugrad = (hgrad * silu).astype(BF16)
    gg_ref[...] = ggrad
    ug_ref[...] = ugrad
    acc_n[...] += dot_nt(ggrad, wg) + dot_nt(ugrad, wu)

    @pl.when(j == pl.num_programs(0) - 1)
    def _():
        out_ref[...] = acc_out[...].astype(BF16)
        ngrad_ref[...] = acc_n[...].astype(BF16)


def mlp(x, own, other, gain, cot, wg, wu, wd):
    rows, width = x.shape
    units = wg.shape[1]
    step = 256 if units % 256 == 0 else 128
    full = whole((rows, width))
    col = pl.BlockSpec((rows, step), lambda j: (0, j))
    wcol = pl.BlockSpec((width, step), lambda j: (0, j))
    sds = jax.ShapeDtypeStruct
    return pl.pallas_call(
        mlp_kernel,
        grid=(units // step,),
        in_specs=[full, full, full, whole((1, width)), full, wcol, wcol,
                  pl.BlockSpec((step, width), lambda j: (j, 0))],
        out_specs=[full, full, col, col, col, full, full],
        out_shape=[
            sds((rows, width), F32), sds((rows, width), BF16),
            sds((rows, units), BF16), sds((rows, units), BF16), sds((rows, units), BF16),
            sds((rows, width), BF16), sds((rows, width), BF16),
        ],
        scratch_shapes=[pltpu.VMEM((rows, width), F32), pltpu.VMEM((rows, width), F32)],
        compiler_params=params(1),
        name="feed_forward",
    )(x, own, other, gain, cot, wg, wu, wd)


def wgrad_kernel(a_ref, b_ref, o_ref):
    o_ref[...] = dot_tn(a_ref[...], b_ref[...]).astype(BF16)


def wgrad(a, b, name):
    rows, m = a.shape
    n = b.shape[1]
    step = 256 if m % 256 == 0 else 128
    return pl.pallas_call(
        wgrad_kernel,
        grid=(m // step,),
        in_specs=[pl.BlockSpec((rows, step), lambda j: (0, j)), whole((rows, n))],
        out_specs=pl.BlockSpec((step, n), lambda j: (j, 0)),
        out_shape=jax.ShapeDtypeStruct((m, n), BF16),
        compiler_params=params(1),
        name=name,
    )(a, b)


def attn_bwd_kernel(
    nown_ref, nother_ref, mid_ref, cot_ref, mgain_ref, n1_ref, al_ref, p_ref, qraw_ref, kraw_ref, qrot_ref,
    krot_ref, v_ref, wq_ref, wk_ref, wv_ref, wo_ref, qg_ref, kg_ref, cos_ref, sin_ref,
    mgrad_ref, mgg_ref, owg_ref, qwg_ref, kwg_ref, vwg_ref, qgg_ref, kgg_ref, n1g_ref, blow, acc,
):
    g = pl.program_id(0)
    rows = mid_ref.shape[0]
    heads = wq_ref.shape[1] // HEAD_SIZE

    @pl.when(g == 0)
    def _():
        ngrad = nown_ref[...].astype(F32) + nother_ref[...].astype(F32)
        middle = mid_ref[...]
        inv = inv_rms(middle)
        u = middle * inv
        mgg_ref[...] = jnp.sum(ngrad * u, 0, keepdims=True)
        s = ngrad * mgain_ref[...]
        mgrad = cot_ref[...].astype(F32) + inv * (s - u * jnp.mean(s * u, -1, keepdims=True))
        mgrad_ref[...] = mgrad
        blow[...] = mgrad.astype(BF16)
        acc[...] = jnp.zeros_like(acc)
        qgg_ref[...] = jnp.zeros_like(qgg_ref)
        kgg_ref[...] = jnp.zeros_like(kgg_ref)

    branch_low = blow[...]
    agrad = dot_nt(branch_low, wo_ref[...]).astype(BF16)
    owg_ref[...] = dot_tn(al_ref[...], branch_low).astype(BF16)
    agrad = jnp.concatenate([agrad[:, h * HEAD_SIZE : (h + 1) * HEAD_SIZE] for h in range(heads)], 0)
    prob = p_ref[0]
    pgrad = dot_nt(agrad, v_ref[...])
    prob_wide = prob.astype(F32)
    row_dot = jnp.sum(pgrad * prob_wide, -1, keepdims=True)
    sgrad = (prob_wide * (pgrad - row_dot)).astype(BF16)
    vgrad = dot_tn(prob, agrad).astype(BF16)
    qrgrad = dot_nn(sgrad, krot_ref[...])
    krgrad = dot_tn(sgrad, qrot_ref[0])
    cosine, sine = cos_ref[...], sin_ref[...]

    def back(raw, gain, grad):
        inv = inv_rms(raw)
        u = raw * inv
        dn = grad * cosine + pltpu.roll(grad * sine, HEAD_SIZE // 2, 1)
        s = dn * gain
        return (
            (inv * (s - u * jnp.mean(s * u, -1, keepdims=True))).astype(BF16),
            jnp.sum(dn * u, 0, keepdims=True),
        )

    scale = HEAD_SIZE ** (-0.5)
    grads = []
    q_raw = qraw_ref[...]
    for h in range(heads):
        qgrad, qgg = back(
            q_raw[:, h * HEAD_SIZE : (h + 1) * HEAD_SIZE], qg_ref[...], qrgrad[h * rows : (h + 1) * rows] * scale
        )
        qgg_ref[...] += qgg
        grads.append(qgrad)
    kgrad, kgg = back(kraw_ref[...], kg_ref[...], krgrad)
    kgg_ref[...] += kgg
    grads += [kgrad, vgrad]
    grads = jnp.concatenate(grads, 1)
    wg = dot_tn(n1_ref[...], grads).astype(BF16)
    qw = heads * HEAD_SIZE
    qwg_ref[...] = wg[:, :qw]
    kwg_ref[...] = wg[:, qw : qw + HEAD_SIZE]
    vwg_ref[...] = wg[:, qw + HEAD_SIZE :]
    acc[...] += dot_nt(grads, jnp.concatenate([wq_ref[...], wk_ref[...], wv_ref[...]], 1))

    @pl.when(g == pl.num_programs(0) - 1)
    def _():
        n1g_ref[...] = acc[...].astype(BF16)


def attn_bwd(nown, nother, middle, cot, mgain, n1, al, prob, qraw, kraw, qrot, krot, v, wq, wk, wv, wo, qg, kg,
             cosine, sine):
    rows, width = middle.shape
    groups = wk.shape[1] // HEAD_SIZE
    heads = wq.shape[1] // wk.shape[1]
    qw = heads * HEAD_SIZE
    full = whole((rows, width))
    col = lambda n: pl.BlockSpec((rows, n), lambda g: (0, g))
    wcol = lambda n: pl.BlockSpec((width, n), lambda g: (0, g))
    wrow = pl.BlockSpec((qw, width), lambda g: (g, 0))
    stack = lambda n: pl.BlockSpec((1, heads * rows, n), lambda g: (g, 0, 0))
    sds = jax.ShapeDtypeStruct
    return pl.pallas_call(
        attn_bwd_kernel,
        grid=(groups,),
        in_specs=[
            full, full, full, full, whole((1, width)), full, col(qw), stack(rows), col(qw), col(HEAD_SIZE),
            stack(HEAD_SIZE), col(HEAD_SIZE), col(HEAD_SIZE), wcol(qw), wcol(HEAD_SIZE), wcol(HEAD_SIZE), wrow,
            whole((1, HEAD_SIZE)), whole((1, HEAD_SIZE)), whole((rows, HEAD_SIZE)), whole((rows, HEAD_SIZE)),
        ],
        out_specs=[
            full, whole((1, width)), wrow, wcol(qw), wcol(HEAD_SIZE), wcol(HEAD_SIZE),
            whole((1, HEAD_SIZE)), whole((1, HEAD_SIZE)), full,
        ],
        out_shape=[
            sds((rows, width), F32), sds((1, width), F32), sds((groups * qw, width), BF16),
            sds((width, groups * qw), BF16), sds((width, groups * HEAD_SIZE), BF16),
            sds((width, groups * HEAD_SIZE), BF16),
            sds((1, HEAD_SIZE), F32), sds((1, HEAD_SIZE), F32), sds((rows, width), BF16),
        ],
        scratch_shapes=[pltpu.VMEM((rows, width), BF16), pltpu.VMEM((rows, width), F32)],
        compiler_params=params(1),
        name="attention_backward",
    )(nown, nother, middle, cot, mgain, n1, al, prob, qraw, kraw, qrot, krot, v, wq, wk, wv, wo, qg, kg,
      cosine, sine)


def swap(x, axis, n, bit):
    return lax.ppermute(x, axis, [(i, i ^ bit) for i in range(n)])


def line_hops(n, stride):
    length = n // stride
    shift = lambda a, b: [(a * stride + r, b * stride + r) for r in range(stride)]
    last = length - 1
    inward = [shift(s, s + 1) + shift(last - s, last - s - 1) for s in range(length // 2 - 1)]
    middle = length // 2
    across = shift(middle - 1, middle) + shift(middle, middle - 1)
    outward = [shift(s + 1, s) + shift(last - s - 1, last - s) for s in reversed(range(length // 2 - 1))]
    return inward, across, outward


def add(a, b):
    return (a.astype(F32) + b.astype(F32)).astype(BF16)


def half_of(x, bit, axis=0):
    size = x.shape[axis] // 2
    return lax.dynamic_slice_in_dim(x, bit * size, size, axis)


def join(bit, own, other):
    return jnp.where(bit == 0, jnp.concatenate([own, other], 0), jnp.concatenate([other, own], 0))


def sum_over_dp(x, n):
    place = lax.axis_index("dp")
    core, pair, spot = place % 2, (place // 2) % 2, place // 4
    x = add(half_of(x, core), swap(half_of(x, 1 - core), "dp", n, 1))
    x = add(half_of(x, pair), swap(half_of(x, 1 - pair), "dp", n, 2))
    inward, across, outward = line_hops(n, 4)
    for hop in inward:
        x = add(x, lax.ppermute(x, "dp", hop))
    x = add(x, lax.ppermute(x, "dp", across))
    for step, hop in enumerate(outward):
        edge = len(outward) - 1 - step
        takes = (spot == edge) | (spot == n // 4 - 1 - edge)
        x = jnp.where(takes, lax.ppermute(x, "dp", hop), x)
    beside = swap(x, "dp", n, 2)
    far, far_beside = swap(x, "dp", n, 1), swap(beside, "dp", n, 1)
    return join(core, join(pair, x, beside), join(pair, far, far_beside)).astype(F32)


def sum_small(x, n, tensor):
    x = x + swap(x, "dp", n, 1)
    x = x + swap(x, "dp", n, 2)
    inward, across, outward = line_hops(n, 4)
    spot = lax.axis_index("dp") // 4
    for hop in inward:
        x = x + lax.ppermute(x, "dp", hop)
    x = x + lax.ppermute(x, "dp", across)
    for step, hop in enumerate(outward):
        edge = len(outward) - 1 - step
        takes = (spot == edge) | (spot == n // 4 - 1 - edge)
        x = jnp.where(takes, lax.ppermute(x, "dp", hop), x)
    return x + swap(x, "tensor", 2, 1) if tensor == 2 else lax.psum(x, "tensor")


def others(x, tensor):
    if tensor == 2:
        return swap(x, "tensor", 2, 1)
    return (lax.psum(x.astype(F32), "tensor") - x.astype(F32)).astype(x.dtype)


def features(x, tensor):
    if tensor == 2:
        other = swap(x, "tensor", 2, 1)
        first = lax.axis_index("tensor") == 0
        return jnp.where(first, jnp.concatenate([x, other], 1), jnp.concatenate([other, x], 1))
    return lax.all_gather(x, "tensor", axis=1, tiled=True)


def per_device(
    dp, tensor, tokens, cotangent, attn_gain, query_weight, key_matrix, value_matrix, query_gain,
    key_norm_gain, out_weight, mlp_gain, gate_weight, up_weight, down_weight,
):
    x = features(tokens, tensor)
    cot = features(cotangent, tensor)
    rows, width = x.shape
    share = tokens.shape[1]
    offset = lax.axis_index("tensor") * share
    mine = lambda a: lax.dynamic_slice_in_dim(a, offset, share, 1)
    cosine, sine = (jnp.asarray(t) for t in rope_tables())
    attn_gain, mlp_gain = attn_gain[None], mlp_gain[None]
    query_gain, key_norm_gain = query_gain[None], key_norm_gain[None]

    n1, qraw, kraw, qrot, krot, v, prob, al, branch, branch_low = attn_fwd(
        x, attn_gain, query_weight, key_matrix, value_matrix, out_weight, query_gain, key_norm_gain, cosine, sine
    )
    middle, n2, hidden, ggrad, ugrad, mlp_part, ngrad = mlp(
        x, branch, others(branch_low, tensor), mlp_gain, cot, gate_weight, up_weight, down_weight
    )
    ngrad_other = others(ngrad, tensor)
    down_wgrad = sum_over_dp(wgrad(hidden, cot, "down_gradient"), dp)
    gate_wgrad = sum_over_dp(wgrad(n2, ggrad, "gate_gradient"), dp)
    up_wgrad = sum_over_dp(wgrad(n2, ugrad, "up_gradient"), dp)
    mgrad, mgg, owg, qwg, kwg, vwg, qgg, kgg, n1g = attn_bwd(
        ngrad, ngrad_other, middle, cot, mlp_gain, n1, al, prob, qraw, kraw, qrot, krot, v,
        query_weight, key_matrix, value_matrix, out_weight, query_gain, key_norm_gain, cosine, sine,
    )
    out_wgrad = sum_over_dp(owg, dp)
    query_wgrad = sum_over_dp(qwg, dp)
    kv_wgrad = sum_over_dp(jnp.concatenate([kwg, vwg], 1), dp)
    key_wgrad, value_wgrad = kv_wgrad[:, : kwg.shape[1]], kv_wgrad[:, kwg.shape[1] :]

    if tensor == 2:
        t = lax.axis_index("tensor")
        arrived = swap(half_of(mlp_part, 1 - t, 1), "tensor", 2, 1)
        mlp_share = mine(mlp_part).astype(F32) + arrived.astype(F32)
    else:
        mlp_share = lax.psum_scatter(mlp_part, "tensor", scatter_dimension=1, tiled=True).astype(F32)
    layer_out = (mine(middle) + mlp_share).astype(BF16)

    n1_grad = n1g.astype(F32) + others(n1g, tensor).astype(F32)
    wide = x.astype(F32)
    inv_one = inv_rms(wide)
    u = wide * inv_one
    s = n1_grad * attn_gain
    mean = jnp.mean(s * u, -1, keepdims=True)
    input_grad = (mine(mgrad) + inv_one * (mine(s) - mine(u) * mean)).astype(BF16)
    agg = jnp.sum(n1_grad * u, 0, keepdims=True)

    here = jnp.arange(width)[None] // share == lax.axis_index("tensor")
    small = jnp.concatenate([jnp.where(here, agg, 0.0), jnp.where(here, mgg, 0.0), qgg, kgg], 1)
    small = sum_small(small, dp, tensor)[0]
    return (
        layer_out, input_grad, small[:width], query_wgrad, key_wgrad, value_wgrad,
        small[2 * width : 2 * width + HEAD_SIZE], small[2 * width + HEAD_SIZE :], out_wgrad,
        small[width : 2 * width], gate_wgrad, up_wgrad, down_wgrad,
    )


def solution(mesh):
    rows, cols, rep = P("tensor", None), P(None, "tensor"), P()
    both = P("dp", "tensor")
    return jax.shard_map(
        functools.partial(per_device, mesh.shape["dp"], mesh.shape["tensor"]),
        mesh=mesh,
        in_specs=(both, both, rep, cols, cols, cols, rep, rep, rows, rep, cols, cols, rows),
        out_specs=(both, both, rep, cols, cols, cols, rep, rep, rows, rep, cols, cols, rows),
        check_vma=False,
    )
```

```python
import functools

import jax
import jax.numpy as jnp
import numpy as np
from jax import lax
from jax.experimental import pallas as pl
from jax.experimental.pallas import tpu as pltpu
from jax.sharding import PartitionSpec as P

HEAD_SIZE = 128
SEQUENCE_LENGTH = 384
epsilon = 1e-06
rope_base = 1000000.0
F32 = jnp.float32
BF16 = jnp.bfloat16
def dot_nn(a, b):
    return lax.dot_general(a, b, (((1,), (0,)), ((), ())), preferred_element_type=F32)


def dot_nt(a, b):
    return lax.dot_general(a, b, (((1,), (1,)), ((), ())), preferred_element_type=F32)


def dot_tn(a, b):
    return lax.dot_general(a, b, (((0,), (0,)), ((), ())), preferred_element_type=F32)


def rope_tables():
    half = HEAD_SIZE // 2
    frequency = rope_base ** (-np.arange(half, dtype=np.float64) * (2.0 / HEAD_SIZE))
    angle = np.arange(SEQUENCE_LENGTH, dtype=np.float64)[:, None] * frequency[None, :]
    cosine, sine = np.cos(angle), np.sin(angle)
    return (
        np.concatenate([cosine, cosine], 1).astype(np.float32),
        np.concatenate([-sine, sine], 1).astype(np.float32),
    )


def inv_rms(v):
    return lax.rsqrt(jnp.mean(v * v, -1, keepdims=True) + epsilon)


def near(x):
    return pltpu.with_memory_space_constraint(x, pltpu.VMEM)


def call(kernel, outs, name, *args, megabytes=24, **more):
    return pl.pallas_call(
        kernel,
        in_specs=[pl.BlockSpec(memory_space=pltpu.SMEM if a.dtype == jnp.int32 else pltpu.VMEM) for a in args],
        out_specs=[pl.BlockSpec(memory_space=pltpu.VMEM) for _ in outs],
        out_shape=[pltpu.VMEM(shape, kind) for shape, kind in outs],
        compiler_params=pltpu.CompilerParams(vmem_limit_bytes=megabytes * 1024 * 1024),
        name=name,
        **more,
    )(*(a if a.dtype == jnp.int32 else near(a) for a in args))


def join(side, own_ref, got_ref, out_ref):
    share = own_ref.shape[1]
    out_ref[:, pl.ds(pl.multiple_of(side * share, share), share)] = own_ref[...]
    out_ref[:, pl.ds(pl.multiple_of((1 - side) * share, share), share)] = got_ref[...]


def attn_fwd_kernel(
    halves, ids_ref, gain_ref, wq_ref, wk_ref, wv_ref, wo_ref, qg_ref, kg_ref, cos_ref, sin_ref, *refs
):
    ins, refs = refs[: 1 + halves], refs[1 + halves :]
    if halves:
        x_ref, refs = refs[0], refs[1:]
        join(ids_ref[2], *ins, x_ref)
    else:
        (x_ref,) = ins
    n1_ref, qraw_ref, kraw_ref, qrot_ref, krot_ref, v_ref, p_ref, al_ref, branch_ref = refs
    rows = x_ref.shape[0]
    groups = wk_ref.shape[1] // HEAD_SIZE
    heads = wq_ref.shape[1] // wk_ref.shape[1]
    x = x_ref[...].astype(F32)
    n1 = (x * inv_rms(x) * gain_ref[...]).astype(BF16)
    n1_ref[...] = n1
    qraw_ref[...] = dot_nn(n1, wq_ref[...])
    kraw_ref[...] = dot_nn(n1, wk_ref[...])
    v_ref[...] = dot_nn(n1, wv_ref[...]).astype(BF16)
    cosine, sine = cos_ref[...], sin_ref[...]

    def rotate(raw, gain):
        n = raw * inv_rms(raw) * gain
        return n * cosine + pltpu.roll(n, HEAD_SIZE // 2, 1) * sine

    scale = HEAD_SIZE ** (-0.5)
    allowed = lax.broadcasted_iota(jnp.int32, (rows, rows), 1) <= lax.broadcasted_iota(jnp.int32, (rows, rows), 0)
    for g in range(groups):
        kv = slice(g * HEAD_SIZE, (g + 1) * HEAD_SIZE)
        k_rot = rotate(kraw_ref[:, kv], kg_ref[...]).astype(BF16)
        krot_ref[:, kv] = k_rot
        for h in range(heads):
            at = slice((g * heads + h) * HEAD_SIZE, (g * heads + h + 1) * HEAD_SIZE)
            here = slice(h * rows, (h + 1) * rows)
            q_rot = (rotate(qraw_ref[:, at], qg_ref[...]) * scale).astype(BF16)
            qrot_ref[g, here, :] = q_rot
            scores = jnp.where(allowed, dot_nt(q_rot, k_rot), -1e30)
            raised = jnp.exp(scores - jnp.max(scores, -1, keepdims=True))
            prob = (raised * (1.0 / jnp.sum(raised, -1, keepdims=True))).astype(BF16)
            p_ref[g, here, :] = prob
            al_ref[:, at] = dot_nn(prob, v_ref[:, kv]).astype(BF16)
    branch_ref[...] = dot_nn(al_ref[...], wo_ref[...]).astype(BF16)


def attn_fwd(ids, xs, attn_gain, wq, wk, wv, wo, q_gain, k_gain, cosine, sine):
    rows, width = xs[0].shape[0], wq.shape[0]
    groups = wk.shape[1] // HEAD_SIZE
    heads = wq.shape[1] // wk.shape[1]
    full, kv, q = (rows, width), (rows, wk.shape[1]), (rows, wq.shape[1])
    outs = [(full, BF16), (q, F32), (kv, F32), ((groups, heads * rows, HEAD_SIZE), BF16), (kv, BF16), (kv, BF16),
            ((groups, heads * rows, rows), BF16), (q, BF16), (full, BF16)]
    if len(xs) == 2:
        outs = [(full, BF16)] + outs
    out = call(
        functools.partial(attn_fwd_kernel, len(xs) - 1), outs, "attention_forward",
        ids, attn_gain, wq, wk, wv, wo, q_gain, k_gain, cosine, sine, *xs,
    )
    return out if len(xs) == 2 else [xs[0], *out]


def mlp_kernel(halves, ids_ref, x_ref, own_ref, other_ref, gain_ref, wg_ref, wu_ref, wd_ref, *refs):
    ins, refs = refs[: 1 + halves], refs[1 + halves :]
    if halves:
        cot_ref, refs = refs[0], refs[1:]
        join(ids_ref[2], *ins, cot_ref)
    else:
        (cot_ref,) = ins
    mid_ref, n2_ref, hid_ref, gg_ref, ug_ref, out_ref, ngrad_ref = refs
    middle = x_ref[...].astype(F32) + (own_ref[...].astype(F32) + other_ref[...].astype(F32))
    mid_ref[...] = middle
    n2 = (middle * inv_rms(middle) * gain_ref[...]).astype(BF16)
    n2_ref[...] = n2
    units = wg_ref.shape[1]
    step = 512 if units % 512 == 0 else units
    for j in range(0, units, step):
        at = slice(j, j + step)
        gate = dot_nn(n2, wg_ref[:, at])
        up = dot_nn(n2, wu_ref[:, at])
        hgrad = dot_nt(cot_ref[...], wd_ref[at, :])
        sig = jax.nn.sigmoid(gate)
        silu = gate * sig
        hid_ref[:, at] = (silu * up).astype(BF16)
        gg_ref[:, at] = (hgrad * up * sig * (1.0 + gate * (1.0 - sig))).astype(BF16)
        ug_ref[:, at] = (hgrad * silu).astype(BF16)
    ngrad_ref[...] = (dot_nt(gg_ref[...], wg_ref[...]) + dot_nt(ug_ref[...], wu_ref[...])).astype(BF16)
    out_ref[...] = dot_nn(hid_ref[...], wd_ref[...]).astype(BF16)


def mlp(ids, x, own, other, gain, wg, wu, wd, cots):
    full, hid = x.shape, (x.shape[0], wg.shape[1])
    outs = [(full, F32), (full, BF16), (hid, BF16), (hid, BF16), (hid, BF16), (full, BF16), (full, BF16)]
    if len(cots) == 2:
        outs = [(full, BF16)] + outs
    out = call(functools.partial(mlp_kernel, len(cots) - 1), outs, "feed_forward",
               ids, x, own, other, gain, wg, wu, wd, *cots)
    return out if len(cots) == 2 else [cots[0], *out]


def quarter(r, ids):
    core = 1 - ids[0] if r < 2 else ids[0]
    return 2 * core + (1 - ids[1] if r % 2 == 0 else ids[1])


def pieces_kernel(layouts, ids_ref, *refs):
    n = sum(len(layout) for _, layout in layouts)
    ins, outs = refs[: 2 * n], refs[2 * n :]
    i = 0
    for (base, layout), out_ref in zip(layouts, outs):
        for wide, begin, row, fold, lane in layout:
            a_ref, b_ref = ins[2 * i], ins[2 * i + 1]
            i += 1
            size = a_ref.shape[1] // 4
            for r in range(2):
                at = pl.multiple_of(quarter(base + r, ids_ref) * size, size)
                w = dot_tn(a_ref[:, pl.ds(at, size)], b_ref[:, begin : begin + wide]).astype(BF16)
                high = size // fold
                for f in range(fold):
                    lanes = slice(lane + f * wide, lane + (f + 1) * wide)
                    out_ref[r, row : row + high, lanes] = w[f * high : (f + 1) * high]


def pieces(ids, chunks, name):
    layouts = tuple((base, tuple(part[2:] for part in parts)) for base, parts, _, _ in chunks)
    args = [x for _, parts, _, _ in chunks for part in parts for x in part[:2]]
    outs = [((2, rows, width), BF16) for _, _, rows, width in chunks]
    return call(functools.partial(pieces_kernel, layouts), outs, name, ids, *args)


def place_kernel(layout, n, ids_ref, *refs):
    outs = refs[-len(layout) :]
    i = pl.program_id(0)

    def spread(piece):
        for out_ref, segments in zip(outs, layout):
            for row, high, fold, lane, wide, to in segments:
                h = high // fold
                for f in range(fold):
                    lanes = slice(lane + f * wide, lane + (f + 1) * wide)
                    out_ref[f * h : (f + 1) * h, to : to + wide] = piece[row : row + h, lanes].astype(F32)

    for k in range(n):
        pl.when(i == k)(functools.partial(lambda ref: spread(ref[...]), refs[k]))


def home(r, ids):
    core = jnp.where(r < 2, ids[0], 1 - ids[0])
    return 2 * core + jnp.where(r % 2 == 0, ids[1], 1 - ids[1])


def place(ids, base, sources, outs, name, earlier=None):
    earlier = earlier or [None] * len(outs)
    extra = [e for e in earlier if e is not None]
    n = len(sources)
    to = [k for k, e in enumerate(earlier) if e is not None]
    return pl.pallas_call(
        functools.partial(place_kernel, tuple(o[4] for o in outs), n),
        grid_spec=pltpu.PrefetchScalarGridSpec(
            num_scalar_prefetch=1,
            grid=(n,),
            in_specs=[pl.BlockSpec(memory_space=pltpu.VMEM)] * n + [pl.BlockSpec(memory_space=pl.ANY)] * len(extra),
            out_specs=[
                pl.BlockSpec((o[0], o[1]), functools.partial(lambda k, i, ids: (home(base + i, ids), k), o[2])) for o in outs
            ],
        ),
        out_shape=[jax.ShapeDtypeStruct((4 * o[0], o[3]), F32) for o in outs],
        input_output_aliases={1 + n + e: k for e, k in enumerate(to)},
        compiler_params=pltpu.CompilerParams(dimension_semantics=("arbitrary",), vmem_limit_bytes=24 * 1024 * 1024),
        name=name,
    )(ids, *(near(s) for s in sources), *extra)


def attn_bwd_kernel(
    first, last, begin, end, p_ref, qraw_ref, kraw_ref, qrot_ref, krot_ref, v_ref, wq_ref, wk_ref, wv_ref, wo_ref,
    qg_ref, kg_ref, cos_ref, sin_ref, *refs
):
    rows = kraw_ref.shape[0]
    heads = wq_ref.shape[1] // wk_ref.shape[1]
    if first:
        nown_ref, nother_ref, mid_ref, cot_ref, mgain_ref, *refs = refs
        mgrad_ref, mgg_ref, blow_ref, *refs = refs
        ngrad = nown_ref[...].astype(F32) + nother_ref[...].astype(F32)
        middle = mid_ref[...]
        inv = inv_rms(middle)
        u = middle * inv
        mgg_ref[...] = jnp.sum(ngrad * u, 0, keepdims=True)
        s = ngrad * mgain_ref[...]
        mgrad = cot_ref[...].astype(F32) + inv * (s - u * jnp.mean(s * u, -1, keepdims=True))
        mgrad_ref[...] = mgrad
        blow_ref[...] = mgrad.astype(BF16)
    else:
        blow_ref, acc_ref, gains_ref, *refs = refs
    qgrad_ref, kgrad_ref, vgrad_ref, *refs = refs
    q_at = slice(begin * heads * HEAD_SIZE, end * heads * HEAD_SIZE)
    kv_at = slice(begin * HEAD_SIZE, end * HEAD_SIZE)
    cosine, sine = cos_ref[...], sin_ref[...]
    scale = HEAD_SIZE ** (-0.5)
    agrads = dot_nt(blow_ref[...], wo_ref[q_at, :]).astype(BF16)

    def back(raw, gain, grad):
        inv = inv_rms(raw)
        u = raw * inv
        dn = grad * cosine + pltpu.roll(grad * sine, HEAD_SIZE // 2, 1)
        s = dn * gain
        return (
            (inv * (s - u * jnp.mean(s * u, -1, keepdims=True))).astype(BF16),
            jnp.sum(dn * u, 0, keepdims=True),
        )

    qgg = jnp.zeros((1, HEAD_SIZE), F32)
    kgg = jnp.zeros((1, HEAD_SIZE), F32)
    for g in range(begin, end):
        kv = slice(g * HEAD_SIZE, (g + 1) * HEAD_SIZE)
        out = slice((g - begin) * HEAD_SIZE, (g - begin + 1) * HEAD_SIZE)
        krgrad, vgrad = 0.0, 0.0
        for h in range(heads):
            here = slice(h * rows, (h + 1) * rows)
            n = (g - begin) * heads + h
            at = slice(n * HEAD_SIZE, (n + 1) * HEAD_SIZE)
            agrad = agrads[:, at]
            prob = p_ref[g, here, :]
            prob_wide = prob.astype(F32)
            pgrad = dot_nt(agrad, v_ref[:, kv])
            sgrad = (prob_wide * (pgrad - jnp.sum(pgrad * prob_wide, -1, keepdims=True))).astype(BF16)
            vgrad += dot_tn(prob, agrad)
            krgrad += dot_tn(sgrad, qrot_ref[g, here, :])
            raw = qraw_ref[:, (g * heads + h) * HEAD_SIZE : (g * heads + h + 1) * HEAD_SIZE]
            qgrad, part = back(raw, qg_ref[...], dot_nn(sgrad, krot_ref[:, kv]) * scale)
            qgrad_ref[:, at] = qgrad
            qgg += part
        kgrad, part = back(kraw_ref[:, kv], kg_ref[...], krgrad)
        kgrad_ref[:, out] = kgrad
        vgrad_ref[:, out] = vgrad.astype(BF16)
        kgg += part
    total = (
        dot_nt(qgrad_ref[...], wq_ref[:, q_at]) + dot_nt(kgrad_ref[...], wk_ref[:, kv_at])
        + dot_nt(vgrad_ref[...], wv_ref[:, kv_at])
    )
    width = total.shape[1]
    gains = jnp.concatenate([qgg, kgg, jnp.zeros((1, width - 2 * HEAD_SIZE), F32)], 1)
    gains = jnp.concatenate([gains, jnp.zeros((15, width), F32)], 0)
    if not first:
        total += acc_ref[...]
        gains += gains_ref[...]
    if last:
        (n1g_ref,) = refs
        n1g_ref[:rows] = total.astype(BF16)
        n1g_ref[rows:] = gains.astype(BF16)
    else:
        acc_out, gains_out = refs
        acc_out[...] = total
        gains_out[...] = gains


def attn_bwd(common, begin, end, first, last, *more):
    rows, width = common[2].shape[0], common[6].shape[0]
    heads = common[6].shape[1] // common[7].shape[1]
    full = (rows, width)
    n = (end - begin) * HEAD_SIZE
    outs = [(full, F32), ((1, width), F32), (full, BF16)] if first else []
    outs += [((rows, heads * n), BF16), ((rows, n), BF16), ((rows, n), BF16)]
    outs += [((rows + 16, width), BF16)] if last else [(full, F32), ((16, width), F32)]
    return call(functools.partial(attn_bwd_kernel, first, last, begin, end), outs, "attention_backward", *common, *more)


def swap_pairs(n, bit):
    return [(i, i ^ bit) for i in range(n)]


def line_hops(n):
    step = n // 4
    shift = lambda a, b: [(a * step + r, b * step + r) for r in range(step)]
    return shift(0, 1) + shift(3, 2), shift(1, 2) + shift(2, 1), shift(1, 0) + shift(2, 3)


def add(a, b):
    return (a.astype(F32) + b.astype(F32)).astype(BF16)


def others(x, tensor):
    if tensor == 2:
        return lax.ppermute(x, "tensor", swap_pairs(2, 1))
    return (lax.psum(x.astype(F32), "tensor") - x.astype(F32)).astype(x.dtype)


def features(x, tensor):
    if tensor == 2:
        return x, lax.ppermute(x, "tensor", swap_pairs(2, 1))
    return (lax.all_gather(x, "tensor", axis=1, tiled=True),)


class Order:
    def __init__(self):
        self.last = None

    def __call__(self, step, *inputs):
        if self.last is not None:
            inputs, _ = lax.optimization_barrier((inputs, self.last))
        out = step(*inputs)
        self.last = jax.tree.leaves(out)[0]
        return out


def per_device(
    dp, tensor, tokens, cotangent, attn_gain, query_weight, key_matrix, value_matrix, query_gain,
    key_norm_gain, out_weight, mlp_gain, gate_weight, up_weight, down_weight,
):
    rows, share = tokens.shape
    width = query_weight.shape[0]
    groups = key_matrix.shape[1] // HEAD_SIZE
    side = lax.axis_index("tensor")
    offset = side * share
    mine = lambda a: lax.dynamic_slice_in_dim(a, offset, share, 1)
    where = lax.axis_index("dp")
    core, pair, spot = where % 2, (where // 2) % 2, where // 4
    ids = jnp.stack([core, pair, side]).astype(jnp.int32)
    cosine, sine = (jnp.asarray(t) for t in rope_tables())
    attn_gain, mlp_gain = attn_gain[None], mlp_gain[None]
    query_gain, key_norm_gain = query_gain[None], key_norm_gain[None]

    order = Order()
    xs = order(lambda *a: a, *features(tokens, tensor))
    cots = features(order(lambda a: (a,), cotangent)[0], tensor)
    x, n1, qraw, kraw, qrot, krot, v, prob, al, branch = order(
        lambda *a: attn_fwd(ids, a, attn_gain, query_weight, key_matrix, value_matrix, out_weight, query_gain,
                            key_norm_gain, cosine, sine), *xs)
    *cots, branch = order(lambda *a: a, *cots, branch)
    cot, middle, n2, hidden, ggrad, ugrad, mlp_part, ngrad = order(
        lambda own, other, *c: mlp(ids, x, own, other, mlp_gain, gate_weight, up_weight, down_weight, c),
        branch, others(branch, tensor), *cots)
    common = (prob, qraw, kraw, qrot, krot, v, query_weight, key_matrix, value_matrix, out_weight, query_gain,
              key_norm_gain, cosine, sine)

    def ending(n1g, arrived, mgrad, mgg):
        n1_grad = n1g[:rows].astype(F32) + arrived[:rows].astype(F32)
        heads = n1g[rows : rows + 1].astype(F32) + arrived[rows : rows + 1].astype(F32)
        wide = x.astype(F32)
        inv_one = inv_rms(wide)
        u = wide * inv_one
        s = n1_grad * attn_gain
        mean = jnp.mean(s * u, -1, keepdims=True)
        input_grad = (mine(mgrad) + inv_one * (mine(s) - mine(u) * mean)).astype(BF16)
        return input_grad, jnp.concatenate([jnp.sum(n1_grad * u, 0, keepdims=True), mgg, heads], 0)

    if tensor != 2 or dp != 16:
        mgrad, mgg, blow, qgrad, kgrad, vgrad, n1g = attn_bwd(
            common, 0, groups, True, True, ngrad, others(ngrad, tensor), middle, cot, mlp_gain)
        input_grad, gains = ending(n1g, others(n1g, tensor), mgrad, mgg)
        total = lambda a: lax.psum(a.astype(BF16), "dp").astype(F32)
        agg, mgg, heads = total(lax.pmean(gains, "tensor"))
        layer_out = (mine(middle) + lax.psum_scatter(mlp_part, "tensor", scatter_dimension=1, tiled=True)).astype(BF16)
        return (
            layer_out, input_grad, agg, total(dot_tn(n1, qgrad)), total(dot_tn(n1, kgrad)), total(dot_tn(n1, vgrad)),
            heads[:HEAD_SIZE], heads[HEAD_SIZE : 2 * HEAD_SIZE], total(dot_tn(al, blow)), mgg,
            total(dot_tn(n2, ggrad)), total(dot_tn(n2, ugrad)), total(dot_tn(hidden, cot)),
        )

    edge = (spot == 0) | (spot == 3)
    inward, across, outward = line_hops(dp)
    between = inward + outward
    send = lambda x, hops: lax.ppermute(x, "dp", hops)
    over_core = lambda x: send(x, swap_pairs(dp, 1))
    over_pair = lambda x: send(x, swap_pairs(dp, 2))
    over_tensor = lambda x: lax.ppermute(x, "tensor", swap_pairs(2, 1))
    half = lambda a, b: lax.dynamic_slice_in_dim(a, b * share, share, 1)
    first = lambda keep, got: (add(keep[0], got[0]), add(keep[1], got[1]))
    same = lambda *a: a

    units, wide = gate_weight.shape[1], qraw.shape[1]
    high, low, thin = width // 4, width // 8, wide // 2
    size = hidden.shape[1] // 4
    rest = units - width

    def hidden_parts(a, b):
        return [(a, b, width, 0, 0, 1, 0), (a, b, rest, width, high, 2, 0)]

    hidden_outs = [(high, units, 0, units, ((0, high, 1, 0, width, 0), (high, high, 2, 0, rest, width)))]
    down_outs = [(size, width, 0, width, ((0, size, 1, 0, width, 0),))]

    nother = over_tensor(ngrad)
    send_d, keep_d = order(lambda h, c: pieces(ids, [(base, [(h, c, width, 0, 0, 1, 0)], size, width) for base in (0, 2)],
                                               "down_gradient"), hidden, cot)
    got_d = over_core(send_d)
    send_g, send_u = order(
        lambda n2, g, u: pieces(ids, [(0, hidden_parts(n2, g), size, width), (0, hidden_parts(n2, u), size, width)],
                                "gate_up_gradient_sent"), n2, ggrad, ugrad)
    x_d, d = order(first, keep_d, got_d)
    pair_d = over_pair(x_d)
    got_g, got_u = over_core(send_g), over_core(send_u)
    keep_g, keep_u = order(
        lambda n2, g, u: pieces(ids, [(2, hidden_parts(n2, g), size, width), (2, hidden_parts(n2, u), size, width)],
                                "gate_up_gradient_kept"), n2, ggrad, ugrad)
    x_g, g, x_u, u = order(lambda a, b, c, d: (*first(a, b), *first(c, d)), keep_g, got_g, keep_u, got_u)
    halfway = groups // 2
    mgrad, mgg, blow, qgrad, kgrad, vgrad, acc, head_gains = order(
        lambda *a: attn_bwd(common, 0, halfway, True, False, *a), ngrad, nother, middle, cot, mlp_gain)
    pair_d, x_g = order(same, pair_d, x_g)
    pair_g = over_pair(x_g)
    (d,) = order(lambda a, b: (add(a, b),), d, pair_d)
    line_d = send(d, inward)
    qgrad2, kgrad2, vgrad2, n1g = order(
        lambda *a: attn_bwd(common, halfway, groups, False, True, *a), blow, acc, head_gains)
    some = halfway * HEAD_SIZE

    def out_parts(al, blow, n1, qgrad):
        return [(al, blow, width, 0, 0, 1, 0), (n1, qgrad, thin, 0, high, 2, 0)]

    def kv_parts(n1, kgrad, kgrad2, vgrad, vgrad2, qgrad2):
        return [(n1, kgrad, some, 0, 0, 1, 0), (n1, kgrad2, some, 0, 0, 1, some), (n1, vgrad, some, 0, 0, 1, 2 * some),
                (n1, vgrad2, some, 0, 0, 1, 3 * some), (n1, qgrad2, thin, 0, high, 2, 0)]

    send_o, send_k = order(
        lambda al, blow, n1, qgrad, *a: pieces(ids, [(0, out_parts(al, blow, n1, qgrad), high + low, width),
                                                     (0, kv_parts(n1, *a), high + low, width)], "attention_gradient_sent"),
        al, blow, n1, qgrad, kgrad, kgrad2, vgrad, vgrad2, qgrad2)
    got_o, got_k = over_core(send_o), over_core(send_k)
    keep_o, keep_k = order(
        lambda al, blow, n1, qgrad, *a: pieces(ids, [(2, out_parts(al, blow, n1, qgrad), high + low, width),
                                                     (2, kv_parts(n1, *a), high + low, width)], "attention_gradient_kept"),
        al, blow, n1, qgrad, kgrad, kgrad2, vgrad, vgrad2, qgrad2)
    x_o, o, x_k, k = order(lambda a, b, c, d: (*first(a, b), *first(c, d)), keep_o, got_o, keep_k, got_k)
    pair_g, x_u = order(same, pair_g, x_u)
    pair_u = over_pair(x_u)
    d, g, mlp_half = order(
        lambda d, line, g, pair, m: (add(d, line), add(g, pair), half(m, 1 - side)), d, line_d, g, pair_g, mlp_part)
    mid_d, line_g = send(d, across), send(g, inward)
    mlp_got = over_tensor(mlp_half)
    pair_u, x_o = order(same, pair_u, x_o)
    pair_o = over_pair(x_o)

    def layer(middle, part, got):
        return (mine(middle) + (mine(part).astype(F32) + got.astype(F32))).astype(BF16)

    layer_out = order(layer, middle, mlp_part, mlp_got)

    def turn(kept, line, inner, mid, new, pair):
        inner = add(inner, mid)
        new = add(new, pair)
        return jnp.where(edge, new, inner), add(kept, line), inner, new

    step, g, d, u = order(turn, g, line_g, d, mid_d, u, pair_u)
    line_du, mid_g = send(step, between), send(g, across)
    arrived = over_tensor(n1g)
    pair_o, x_k = order(same, pair_o, x_k)
    pair_k = over_pair(x_k)

    def z(out, line, new, inner, mid, newest, pair):
        inner = add(inner, mid)
        newest = add(newest, pair)
        return jnp.where(edge, newest, inner), add(new, line), jnp.where(edge, line, out), inner, newest

    step, u, d, g, o = order(z, d, line_du, u, g, mid_g, o, pair_o)
    line_go, mid_u = send(step, between), send(u, across)
    pair_k, d = order(same, pair_k, d)
    near_d = over_pair(d)
    input_grad, gains = order(ending, n1g, arrived, mgrad, mgg)

    def z_last(out, line, new, inner, mid, newest, pair, gains):
        inner = add(inner, mid)
        newest = jnp.concatenate([add(newest, pair), jnp.pad(gains, ((0, 13), (0, 0))).astype(BF16)], 0)
        step = jnp.where(edge, newest, jnp.pad(inner, ((0, 16), (0, 0))))
        return step, add(new, line), jnp.where(edge, line, out), inner, newest

    step, o, g, u, k = order(z_last, g, line_go, o, u, mid_u, k, pair_k, gains)
    line_uk, mid_o = send(step, between), send(o, across)
    near_d, g = order(same, near_d, g)
    near_g = over_pair(g)
    far_d, far_near_d = over_core(d), over_core(near_d)
    u, k, o = order(lambda u, line, k, o, mid: (jnp.where(edge, line[: high + low], u), add(k, line), add(o, mid)),
                    u, line_uk, k, o, mid_o)
    line_o, mid_k = send(o, outward), send(k, across)
    near_g, u = order(same, near_g, u)
    near_u = over_pair(u)
    far_g, far_near_g = over_core(g), over_core(near_g)
    (down_wgrad,) = order(lambda *a: place(ids, 0, a, down_outs, "down_place"), d, near_d, far_d, far_near_d)
    o, k = order(lambda o, line, k, mid: (jnp.where(edge, line, o), add(k, mid)), o, line_o, k, mid_k)
    line_k = send(k, outward)
    near_u, o = order(same, near_u, o)
    near_o = over_pair(o)
    far_u, far_near_u = over_core(u), over_core(near_u)
    (gate_wgrad,) = order(lambda *a: place(ids, 0, a, hidden_outs, "gate_place"), g, near_g, far_g, far_near_g)
    k = order(lambda k, line: jnp.where(edge, line, k), k, line_k)
    near_o, k = order(same, near_o, k)
    near_k = over_pair(k)
    far_o, far_near_o, far_k = over_core(o), over_core(near_o), over_core(k)
    (up_wgrad,) = order(lambda *a: place(ids, 0, a, hidden_outs, "up_place"), u, near_u, far_u, far_near_u)
    out_wgrad, query_wgrad = order(
        lambda *a: place(
            ids, 0, a, [(high, width, 0, width, ((0, high, 1, 0, width, 0),)),
                        (high, thin, 0, wide, ((high, high, 2, 0, thin, 0),))], "out_query_place"),
        o, near_o, far_o, far_near_o)
    last_outs = [
        (high, thin, 0, thin, ((0, high, 1, 0, thin, 0),)), (high, thin, 0, thin, ((0, high, 1, thin, thin, 0),)),
        (high, thin, 1, wide, ((high, high, 2, 0, thin, 0),)), (16, width, 0, width, ((high + low, 16, 1, 0, width, 0),))]
    key_wgrad, value_wgrad, query_wgrad, gains = order(
        lambda k, q: place(ids, 0, [k], last_outs, "own_place", [None, None, q, None]), k, query_wgrad)
    (near_k,) = order(lambda a: (a,), near_k)
    far_near_k = over_core(near_k)
    key_wgrad, value_wgrad, query_wgrad, gains = order(
        lambda a, b, *e: place(ids, 1, [a, b], last_outs, "beside_place", e), near_k, far_k, key_wgrad, value_wgrad,
        query_wgrad, gains)
    key_wgrad, value_wgrad, query_wgrad, gains = order(
        lambda a, *e: place(ids, 3, [a], last_outs, "far_place", e), far_near_k, key_wgrad, value_wgrad, query_wgrad, gains)
    gains = gains.reshape(4, 16, width).sum(0)
    return (
        layer_out, input_grad, gains[0], query_wgrad, key_wgrad, value_wgrad,
        gains[2, :HEAD_SIZE], gains[2, HEAD_SIZE : 2 * HEAD_SIZE], out_wgrad,
        gains[1], gate_wgrad, up_wgrad, down_wgrad,
    )


def solution(mesh):
    rows, cols, rep = P("tensor", None), P(None, "tensor"), P()
    both = P("dp", "tensor")
    return jax.shard_map(
        functools.partial(per_device, mesh.shape["dp"], mesh.shape["tensor"]),
        mesh=mesh,
        in_specs=(both, both, rep, cols, cols, cols, rep, rep, rows, rep, cols, cols, rows),
        out_specs=(both, both, rep, cols, cols, cols, rep, rep, rows, rep, cols, cols, rows),
        check_vma=False,
    )
```

```python
import functools

import jax
import jax.numpy as jnp
import numpy as np
from jax import lax
from jax.experimental import pallas as pl
from jax.experimental.pallas import tpu as pltpu
from jax.sharding import PartitionSpec as P

HEAD_SIZE = 128
SEQUENCE_LENGTH = 384
epsilon = 1e-06
rope_base = 1000000.0
F32 = jnp.float32
BF16 = jnp.bfloat16
def dot_nn(a, b):
    return lax.dot_general(a, b, (((1,), (0,)), ((), ())), preferred_element_type=F32)


def dot_nt(a, b):
    return lax.dot_general(a, b, (((1,), (1,)), ((), ())), preferred_element_type=F32)


def dot_tn(a, b):
    return lax.dot_general(a, b, (((0,), (0,)), ((), ())), preferred_element_type=F32)


def rope_tables():
    half = HEAD_SIZE // 2
    frequency = rope_base ** (-np.arange(half, dtype=np.float64) * (2.0 / HEAD_SIZE))
    angle = np.arange(SEQUENCE_LENGTH, dtype=np.float64)[:, None] * frequency[None, :]
    cosine, sine = np.cos(angle), np.sin(angle)
    return (
        np.concatenate([cosine, cosine], 1).astype(np.float32),
        np.concatenate([-sine, sine], 1).astype(np.float32),
    )


def inv_rms(v):
    return lax.rsqrt(jnp.mean(v * v, -1, keepdims=True) + epsilon)


def near(x):
    return pltpu.with_memory_space_constraint(x, pltpu.VMEM)


def call(kernel, outs, name, *args, anywhere=(), far_outs=(), megabytes=14, **more):
    place = lambda a: a if a.dtype == jnp.int32 else near(a)
    return pl.pallas_call(
        kernel,
        in_specs=[pl.BlockSpec(memory_space=pltpu.SMEM if a.dtype == jnp.int32 else pltpu.VMEM) for a in args]
        + [pl.BlockSpec(memory_space=pltpu.HBM) for _ in anywhere],
        out_specs=[pl.BlockSpec(memory_space=pltpu.VMEM) for _ in outs]
        + [pl.BlockSpec(memory_space=pltpu.HBM) for _ in far_outs],
        out_shape=[pltpu.VMEM(shape, kind) for shape, kind in outs]
        + [pltpu.HBM(shape, kind) for shape, kind in far_outs],
        compiler_params=pltpu.CompilerParams(vmem_limit_bytes=megabytes * 1024 * 1024),
        name=name,
        **more,
    )(*(place(a) for a in args), *(pltpu.with_memory_space_constraint(a, pltpu.HBM) for a in anywhere))


def fetch(sources, targets, sem):
    copies = [pltpu.make_async_copy(s, t, sem.at[i]) for i, (s, t) in enumerate(zip(sources, targets))]
    for copy in copies:
        copy.start()
    return copies


def join(side, ins, out_ref, sem):
    if len(ins) == 1:
        return [pltpu.make_async_copy(ins[0], out_ref, sem.at[0])]
    share = ins[0].shape[1]
    places = [pl.ds(pl.multiple_of(half * share, share), share) for half in (side, 1 - side)]
    return [pltpu.make_async_copy(ref, out_ref.at[:, at], sem.at[i]) for i, (ref, at) in enumerate(zip(ins, places))]


def attn_fwd_kernel(
    n, ids_ref, gains_ref, *refs
):
    weights, table_hbm, refs = refs[n : n + 4], refs[n + 4], [*refs[:n], *refs[n + 5 :]]
    x_ref, branch_ref = refs[n : n + 2]
    outs, (n1_ref, qraw_ref, kraw_ref, qrot_ref, krot_ref, v_ref, p_ref, al_ref) = refs[n + 2 : n + 10], refs[n + 10 : n + 18]
    wq_ref, wk_ref, wv_ref, wo_ref, table_ref, sem, weight_sem, out_sem, table_sem = refs[n + 18 :]
    scratch = (n1_ref, qraw_ref, kraw_ref, qrot_ref, krot_ref, v_ref, p_ref, al_ref)
    written = [pltpu.make_async_copy(s, o, out_sem.at[i]) for i, (s, o) in enumerate(zip(scratch, outs))]
    copies = join(ids_ref[2], refs[:n], x_ref, sem)
    for copy in copies:
        copy.start()
    loads = [pltpu.make_async_copy(s, t, weight_sem.at[i])
             for i, (s, t) in enumerate(zip(weights, (wq_ref, wk_ref, wv_ref, wo_ref)))]
    loads[0].start()
    tables = pltpu.make_async_copy(table_hbm, table_ref, table_sem)
    tables.start()
    gain, q_gain, k_gain = gains_ref[0:1, :], gains_ref[2:3, :HEAD_SIZE], gains_ref[2:3, HEAD_SIZE : 2 * HEAD_SIZE]
    for copy in copies:
        copy.wait()
    rows = x_ref.shape[0]
    groups = wk_ref.shape[1] // HEAD_SIZE
    heads = wq_ref.shape[1] // wk_ref.shape[1]
    x = x_ref[...].astype(F32)
    n1 = (x * inv_rms(x) * gain).astype(BF16)
    n1_ref[...] = n1
    loads[0].wait()
    loads[1].start()
    loads[2].start()
    qraw_ref[...] = dot_nn(n1, wq_ref[...])
    loads[1].wait()
    kraw_ref[...] = dot_nn(n1, wk_ref[...])
    loads[2].wait()
    loads[3].start()
    v_ref[...] = dot_nn(n1, wv_ref[...]).astype(BF16)
    for i in (0, 1, 2, 5):
        written[i].start()
    tables.wait()
    cosine, sine = table_ref[:rows, :], table_ref[rows:, :]

    def rotate(raw, gain):
        n = raw * inv_rms(raw) * gain
        return n * cosine + pltpu.roll(n, HEAD_SIZE // 2, 1) * sine

    scale = HEAD_SIZE ** (-0.5)
    allowed = lax.broadcasted_iota(jnp.int32, (rows, rows), 1) <= lax.broadcasted_iota(jnp.int32, (rows, rows), 0)
    for g in range(groups):
        kv = slice(g * HEAD_SIZE, (g + 1) * HEAD_SIZE)
        k_rot = rotate(kraw_ref[:, kv], k_gain).astype(BF16)
        krot_ref[:, kv] = k_rot
        for h in range(heads):
            at = slice((g * heads + h) * HEAD_SIZE, (g * heads + h + 1) * HEAD_SIZE)
            here = slice(h * rows, (h + 1) * rows)
            q_rot = (rotate(qraw_ref[:, at], q_gain) * scale).astype(BF16)
            qrot_ref[g, here, :] = q_rot
            scores = jnp.where(allowed, dot_nt(q_rot, k_rot), -1e30)
            raised = jnp.exp(scores - jnp.max(scores, -1, keepdims=True))
            prob = (raised * (1.0 / jnp.sum(raised, -1, keepdims=True))).astype(BF16)
            p_ref[g, here, :] = prob
            al_ref[:, at] = dot_nn(prob, v_ref[:, kv]).astype(BF16)
    for i in (3, 4, 6, 7):
        written[i].start()
    loads[3].wait()
    branch_ref[...] = dot_nn(al_ref[...], wo_ref[...]).astype(BF16)
    for copy in written:
        copy.wait()


def attn_fwd(ids, xs, gains, wq, wk, wv, wo, tables):
    rows, width = xs[0].shape[0], wq.shape[0]
    groups = wk.shape[1] // HEAD_SIZE
    heads = wq.shape[1] // wk.shape[1]
    full, kv, q = (rows, width), (rows, wk.shape[1]), (rows, wq.shape[1])
    far_outs = [(full, BF16), (q, F32), (kv, F32), ((groups, heads * rows, HEAD_SIZE), BF16), (kv, BF16), (kv, BF16),
                ((groups, heads * rows, rows), BF16), (q, BF16)]
    return call(
        functools.partial(attn_fwd_kernel, len(xs)), [(full, BF16), (full, BF16)], "attention_forward",
        ids, gains, anywhere=(*xs, wq, wk, wv, wo, tables), far_outs=far_outs,
        megabytes=32,
        scratch_shapes=[pltpu.VMEM(*o) for o in far_outs] + [pltpu.VMEM(w.shape, BF16) for w in (wq, wk, wv, wo)]
        + [pltpu.VMEM(tables.shape, F32), pltpu.SemaphoreType.DMA((2,)), pltpu.SemaphoreType.DMA((4,)),
           pltpu.SemaphoreType.DMA((8,)), pltpu.SemaphoreType.DMA],
    )


def mlp_kernel(n, ids_ref, x_ref, own_ref, other_ref, gains_ref, wg_ref, wu_ref, wd_ref, *refs):
    cot_ref, mid_ref, n2_ref, hid_ref, gg_ref, ug_ref, out_ref, ngrad_ref, sem = refs[n:]
    copies = join(ids_ref[2], refs[:n], cot_ref, sem)
    for copy in copies:
        copy.start()
    units = wg_ref.shape[1]
    step = 512 if units % 512 == 0 else units
    middle = x_ref[...].astype(F32) + (own_ref[...].astype(F32) + other_ref[...].astype(F32))
    mid_ref[...] = middle
    n2 = (middle * inv_rms(middle) * gains_ref[1:2, :]).astype(BF16)
    n2_ref[...] = n2
    for copy in copies:
        copy.wait()
    for j in range(0, units, step):
        at = slice(j, j + step)
        gate = dot_nn(n2, wg_ref[:, at])
        up = dot_nn(n2, wu_ref[:, at])
        hgrad = dot_nt(cot_ref[...], wd_ref[at, :])
        sig = jax.nn.sigmoid(gate)
        silu = gate * sig
        hid_ref[:, at] = (silu * up).astype(BF16)
        gg_ref[:, at] = (hgrad * up * sig * (1.0 + gate * (1.0 - sig))).astype(BF16)
        ug_ref[:, at] = (hgrad * silu).astype(BF16)
    ngrad_ref[...] = (dot_nt(gg_ref[...], wg_ref[...]) + dot_nt(ug_ref[...], wu_ref[...])).astype(BF16)
    out_ref[...] = dot_nn(hid_ref[...], wd_ref[...]).astype(BF16)


def mlp(ids, x, own, other, gains, wg, wu, wd, cots):
    full, hid = x.shape, (x.shape[0], wg.shape[1])
    outs = [(full, F32), (full, BF16), (hid, BF16), (hid, BF16), (hid, BF16), (full, BF16), (full, BF16)]
    return call(
        functools.partial(mlp_kernel, len(cots)), [(full, BF16)] + outs, "feed_forward",
        ids, x, own, other, gains, wg, wu, wd, anywhere=cots, scratch_shapes=[pltpu.SemaphoreType.DMA((2,))],
    )


def quarter(r, ids):
    core = 1 - ids[0] if r < 2 else ids[0]
    return 2 * core + (1 - ids[1] if r % 2 == 0 else ids[1])


def pieces_kernel(layouts, ids_ref, *refs):
    n = sum(len(layout) for _, layout in layouts)
    ins, outs = refs[: 2 * n], refs[2 * n :]
    i = 0
    for (base, layout), out_ref in zip(layouts, outs):
        for wide, begin, row, fold, lane in layout:
            a_ref, b_ref = ins[2 * i], ins[2 * i + 1]
            i += 1
            size = a_ref.shape[1] // 4
            for r in range(2):
                at = pl.multiple_of(quarter(base + r, ids_ref) * size, size)
                w = dot_tn(a_ref[:, pl.ds(at, size)], b_ref[:, begin : begin + wide]).astype(BF16)
                high = size // fold
                for f in range(fold):
                    lanes = slice(lane + f * wide, lane + (f + 1) * wide)
                    out_ref[r, row : row + high, lanes] = w[f * high : (f + 1) * high]


def pieces(ids, chunks, name):
    layouts = tuple((base, tuple(part[2:] for part in parts)) for base, parts, _, _ in chunks)
    args = [x for _, parts, _, _ in chunks for part in parts for x in part[:2]]
    outs = [((2, rows, width), BF16) for _, _, rows, width in chunks]
    return call(functools.partial(pieces_kernel, layouts), outs, name, ids, *args)


def place_kernel(layout, n, ids_ref, *refs):
    outs = refs[-len(layout) :]
    i = pl.program_id(0)

    def spread(piece):
        for out_ref, segments in zip(outs, layout):
            for row, high, fold, lane, wide, to in segments:
                h = high // fold
                for f in range(fold):
                    lanes = slice(lane + f * wide, lane + (f + 1) * wide)
                    out_ref[f * h : (f + 1) * h, to : to + wide] = piece[row : row + h, lanes].astype(F32)

    for k in range(n):
        pl.when(i == k)(functools.partial(lambda ref: spread(ref[...]), refs[k]))


def home(r, ids):
    core = jnp.where(r < 2, ids[0], 1 - ids[0])
    return 2 * core + jnp.where(r % 2 == 0, ids[1], 1 - ids[1])


def place(ids, base, sources, outs, name, earlier=None):
    earlier = earlier or [None] * len(outs)
    extra = [e for e in earlier if e is not None]
    n = len(sources)
    to = [k for k, e in enumerate(earlier) if e is not None]
    return pl.pallas_call(
        functools.partial(place_kernel, tuple(o[4] for o in outs), n),
        grid_spec=pltpu.PrefetchScalarGridSpec(
            num_scalar_prefetch=1,
            grid=(n,),
            in_specs=[pl.BlockSpec(memory_space=pltpu.VMEM)] * n + [pl.BlockSpec(memory_space=pl.ANY)] * len(extra),
            out_specs=[
                pl.BlockSpec((o[0], o[1]), functools.partial(lambda k, i, ids: (home(base + i, ids), k), o[2])) for o in outs
            ],
        ),
        out_shape=[jax.ShapeDtypeStruct((4 * o[0], o[3]), F32) for o in outs],
        input_output_aliases={1 + n + e: k for e, k in enumerate(to)},
        compiler_params=pltpu.CompilerParams(dimension_semantics=("arbitrary",), vmem_limit_bytes=24 * 1024 * 1024),
        name=name,
    )(ids, *(near(s) for s in sources), *extra)


def attn_bwd_kernel(heads, gains_ref, nother_ref, *refs):
    n = 14
    outs = refs[n : n + 7]
    bufs, (sem,) = refs[n + 7 : n + 7 + n], refs[n + 7 + n :]
    copies = [pltpu.make_async_copy(s, t, sem.at[i]) for i, (s, t) in enumerate(zip(refs[:n], bufs))]
    nown_ref, mid_ref, cot_ref, wo_ref, table_ref, v_ref, p_ref, krot_ref, qrot_ref, qraw_ref, kraw_ref = bufs[:11]
    wq_ref, wk_ref, wv_ref = bufs[11:]
    mgrad_ref, mgg_ref, blow_ref, qgrad_ref, kgrad_ref, vgrad_ref, n1g_ref = outs
    rows = kraw_ref.shape[0]
    groups = wk_ref.shape[1] // HEAD_SIZE
    q_gain, k_gain = gains_ref[2:3, :HEAD_SIZE], gains_ref[2:3, HEAD_SIZE : 2 * HEAD_SIZE]
    for copy in copies[:4]:
        copy.start()
    for copy in copies[:3]:
        copy.wait()
    for copy in copies[4:7]:
        copy.start()
    ngrad = nown_ref[...].astype(F32) + nother_ref[...].astype(F32)
    middle = mid_ref[...]
    inv = inv_rms(middle)
    u = middle * inv
    mgg_ref[...] = jnp.sum(ngrad * u, 0, keepdims=True)
    s = ngrad * gains_ref[1:2, :]
    mgrad = cot_ref[...].astype(F32) + inv * (s - u * jnp.mean(s * u, -1, keepdims=True))
    mgrad_ref[...] = mgrad
    blow_ref[...] = mgrad.astype(BF16)
    for copy in copies[7:]:
        copy.start()
    scale = HEAD_SIZE ** (-0.5)
    copies[3].wait()
    copies[4].wait()
    cosine, sine = table_ref[:rows, :], table_ref[rows:, :]
    agrads = dot_nt(blow_ref[...], wo_ref[...]).astype(BF16)

    def back(raw, gain, grad):
        inv = inv_rms(raw)
        u = raw * inv
        dn = grad * cosine + pltpu.roll(grad * sine, HEAD_SIZE // 2, 1)
        s = dn * gain
        return (
            (inv * (s - u * jnp.mean(s * u, -1, keepdims=True))).astype(BF16),
            jnp.sum(dn * u, 0, keepdims=True),
        )

    qgg = jnp.zeros((1, HEAD_SIZE), F32)
    kgg = jnp.zeros((1, HEAD_SIZE), F32)
    for copy in copies[5:11]:
        copy.wait()
    for g in range(groups):
        kv = slice(g * HEAD_SIZE, (g + 1) * HEAD_SIZE)
        krgrad, vgrad = 0.0, 0.0
        for h in range(heads):
            here = slice(h * rows, (h + 1) * rows)
            at = slice((g * heads + h) * HEAD_SIZE, (g * heads + h + 1) * HEAD_SIZE)
            agrad = agrads[:, at]
            prob = p_ref[g, here, :]
            prob_wide = prob.astype(F32)
            pgrad = dot_nt(agrad, v_ref[:, kv])
            sgrad = (prob_wide * (pgrad - jnp.sum(pgrad * prob_wide, -1, keepdims=True))).astype(BF16)
            vgrad += dot_tn(prob, agrad)
            krgrad += dot_tn(sgrad, qrot_ref[g, here, :])
            qgrad, part = back(qraw_ref[:, at], q_gain, dot_nn(sgrad, krot_ref[:, kv]) * scale)
            qgrad_ref[:, at] = qgrad
            qgg += part
        kgrad, part = back(kraw_ref[:, kv], k_gain, krgrad)
        kgrad_ref[:, kv] = kgrad
        vgrad_ref[:, kv] = vgrad.astype(BF16)
        kgg += part
    for copy in copies[11:]:
        copy.wait()
    total = (
        dot_nt(qgrad_ref[...], wq_ref[...]) + dot_nt(kgrad_ref[...], wk_ref[...]) + dot_nt(vgrad_ref[...], wv_ref[...])
    )
    width = total.shape[1]
    gains = jnp.concatenate([qgg, kgg, jnp.zeros((1, width - 2 * HEAD_SIZE), F32)], 1)
    gains = jnp.concatenate([gains, jnp.zeros((15, width), F32)], 0)
    n1g_ref[:rows] = total.astype(BF16)
    n1g_ref[rows:] = gains.astype(BF16)


def attn_bwd(nown, nother, middle, cot, gains, weights, prob, qraw, kraw, qrot, krot, v, tables):
    wq, wk, wv, wo = weights
    rows, width = middle.shape
    full = (rows, width)
    outs = [(full, F32), ((1, width), F32), (full, BF16), (qraw.shape, BF16), (kraw.shape, BF16), (kraw.shape, BF16),
            ((rows + 16, width), BF16)]
    streams = (nown, middle, cot, wo, tables, v, prob, krot, qrot, qraw, kraw, wq, wk, wv)
    return call(
        functools.partial(attn_bwd_kernel, wq.shape[1] // wk.shape[1]), outs, "attention_backward",
        gains, nother, anywhere=streams, megabytes=36,
        scratch_shapes=[pltpu.VMEM(a.shape, a.dtype) for a in streams] + [pltpu.SemaphoreType.DMA((len(streams),))],
    )


def swap_pairs(n, bit):
    return [(i, i ^ bit) for i in range(n)]


def line_hops(n):
    step = n // 4
    shift = lambda a, b: [(a * step + r, b * step + r) for r in range(step)]
    return shift(0, 1) + shift(3, 2), shift(1, 2) + shift(2, 1), shift(1, 0) + shift(2, 3)


def add(a, b):
    return (a.astype(F32) + b.astype(F32)).astype(BF16)


def others(x, tensor):
    if tensor == 2:
        return lax.ppermute(x, "tensor", swap_pairs(2, 1))
    return (lax.psum(x.astype(F32), "tensor") - x.astype(F32)).astype(x.dtype)


def features(x, tensor):
    if tensor == 2:
        return x, lax.ppermute(x, "tensor", swap_pairs(2, 1))
    return (lax.all_gather(x, "tensor", axis=1, tiled=True),)


class Order:
    def __init__(self):
        self.last = None

    def __call__(self, step, *inputs):
        if self.last is not None:
            inputs, _ = lax.optimization_barrier((inputs, self.last))
        out = step(*inputs)
        self.last = jax.tree.leaves(out)
        return out


def per_device(
    dp, tensor, tokens, cotangent, attn_gain, query_weight, key_matrix, value_matrix, query_gain,
    key_norm_gain, out_weight, mlp_gain, gate_weight, up_weight, down_weight,
):
    rows, share = tokens.shape
    width = query_weight.shape[0]
    groups = key_matrix.shape[1] // HEAD_SIZE
    side = lax.axis_index("tensor")
    offset = side * share
    mine = lambda a: lax.dynamic_slice_in_dim(a, offset, share, 1)
    where = lax.axis_index("dp")
    core, pair, spot = where % 2, (where // 2) % 2, where // 4
    ids = jnp.stack([core, pair, side]).astype(jnp.int32)
    tables = jnp.asarray(np.concatenate(rope_tables(), 0))
    attn_gain = attn_gain[None]
    heads_gain = jnp.concatenate([query_gain, key_norm_gain, jnp.zeros((width - 2 * HEAD_SIZE,), F32)])[None]
    gains = jnp.concatenate([attn_gain, mlp_gain[None], heads_gain, jnp.zeros((5, width), F32)], 0)

    order = Order()
    xs = features(tokens, tensor)
    xs = order(lambda *a: a, *xs)
    cots = features(order(lambda a: (a,), cotangent)[0], tensor)
    x, branch, n1, qraw, kraw, qrot, krot, v, prob, al = order(
        lambda *a: attn_fwd(ids, a, gains, query_weight, key_matrix, value_matrix, out_weight, tables), *xs)
    *cots, branch = order(lambda *a: a, *cots, branch)
    branch_got = others(branch, tensor)
    cot, middle, n2, hidden, ggrad, ugrad, mlp_part, ngrad = order(
        lambda own, other, *c: mlp(ids, x, own, other, gains, gate_weight, up_weight, down_weight, c),
        branch, branch_got, *cots)
    weights = (query_weight, key_matrix, value_matrix, out_weight)
    common = (gains, weights, prob, qraw, kraw, qrot, krot, v, tables)

    def ending(n1g, arrived, mgrad, mgg):
        n1_grad = n1g[:rows].astype(F32) + arrived[:rows].astype(F32)
        heads = n1g[rows : rows + 1].astype(F32) + arrived[rows : rows + 1].astype(F32)
        wide = x.astype(F32)
        inv_one = inv_rms(wide)
        u = wide * inv_one
        s = n1_grad * attn_gain
        mean = jnp.mean(s * u, -1, keepdims=True)
        input_grad = (mine(mgrad) + inv_one * (mine(s) - mine(u) * mean)).astype(BF16)
        return input_grad, jnp.concatenate([jnp.sum(n1_grad * u, 0, keepdims=True), mgg, heads], 0)

    if tensor != 2 or dp != 16:
        mgrad, mgg, blow, qgrad, kgrad, vgrad, n1g = attn_bwd(
            ngrad, others(ngrad, tensor), middle, cot, *common)
        input_grad, gains = ending(n1g, others(n1g, tensor), mgrad, mgg)
        total = lambda a: lax.psum(a.astype(BF16), "dp").astype(F32)
        agg, mgg, heads = total(lax.pmean(gains, "tensor"))
        layer_out = (mine(middle) + lax.psum_scatter(mlp_part, "tensor", scatter_dimension=1, tiled=True)).astype(BF16)
        return (
            layer_out, input_grad, agg, total(dot_tn(n1, qgrad)), total(dot_tn(n1, kgrad)), total(dot_tn(n1, vgrad)),
            heads[:HEAD_SIZE], heads[HEAD_SIZE : 2 * HEAD_SIZE], total(dot_tn(al, blow)), mgg,
            total(dot_tn(n2, ggrad)), total(dot_tn(n2, ugrad)), total(dot_tn(hidden, cot)),
        )

    edge = (spot == 0) | (spot == 3)
    inward, across, outward = line_hops(dp)
    between = inward + outward
    send = lambda x, hops: lax.ppermute(x, "dp", hops)
    over_core = lambda x: send(x, swap_pairs(dp, 1))
    over_pair = lambda x: send(x, swap_pairs(dp, 2))
    over_tensor = lambda x: lax.ppermute(x, "tensor", swap_pairs(2, 1))
    half = lambda a, b: lax.dynamic_slice_in_dim(a, b * share, share, 1)
    first = lambda keep, got: (add(keep[0], got[0]), add(keep[1], got[1]))
    same = lambda *a: a

    units, wide = gate_weight.shape[1], qraw.shape[1]
    high, low, thin = width // 4, width // 8, wide // 2
    size = hidden.shape[1] // 4
    rest = units - width

    def hidden_parts(a, b):
        return [(a, b, width, 0, 0, 1, 0), (a, b, rest, width, high, 2, 0)]

    hidden_outs = [(high, units, 0, units, ((0, high, 1, 0, width, 0), (high, high, 2, 0, rest, width)))]
    down_outs = [(size, width, 0, width, ((0, size, 1, 0, width, 0),))]

    nother = over_tensor(ngrad)
    send_d, keep_d = order(lambda h, c: pieces(ids, [(base, [(h, c, width, 0, 0, 1, 0)], size, width) for base in (0, 2)],
                                               "down_gradient"), hidden, cot)
    got_d = over_core(send_d)
    send_g, send_u = order(
        lambda n2, g, u: pieces(ids, [(0, hidden_parts(n2, g), size, width), (0, hidden_parts(n2, u), size, width)],
                                "gate_up_gradient_sent"), n2, ggrad, ugrad)
    x_d, d = order(first, keep_d, got_d)
    pair_d = over_pair(x_d)
    got_g, got_u = over_core(send_g), over_core(send_u)
    keep_g, keep_u = order(
        lambda n2, g, u: pieces(ids, [(2, hidden_parts(n2, g), size, width), (2, hidden_parts(n2, u), size, width)],
                                "gate_up_gradient_kept"), n2, ggrad, ugrad)
    x_g, g, x_u, u = order(lambda a, b, c, d: (*first(a, b), *first(c, d)), keep_g, got_g, keep_u, got_u)
    pair_d, nother, x_g = order(same, pair_d, nother, x_g)
    pair_g = over_pair(x_g)
    d, mlp_half = order(lambda a, b, m: (add(a, b), half(m, 1 - side)), d, pair_d, mlp_part)
    line_d, mlp_got = send(d, inward), over_tensor(mlp_half)
    mgrad, mgg, blow, qgrad, kgrad, vgrad, n1g = order(
        lambda *a: attn_bwd(*a, *common), ngrad, nother, middle, cot)

    def out_pieces(al, blow, n1, qgrad):
        parts = [(al, blow, width, 0, 0, 1, 0), (n1, qgrad, thin, 0, high, 2, 0)]
        return pieces(ids, [(base, parts, high + low, width) for base in (0, 2)], "out_query_gradient")

    def kv_pieces(n1, qgrad, kgrad, vgrad):
        parts = [(n1, kgrad, thin, 0, 0, 1, 0), (n1, vgrad, thin, 0, 0, 1, thin), (n1, qgrad, thin, thin, high, 2, 0)]
        return pieces(ids, [(base, parts, high + low, width) for base in (0, 2)], "key_value_query_gradient")

    send_o, keep_o = order(out_pieces, al, blow, n1, qgrad)
    line_d, pair_g, x_u, send_o = order(same, line_d, pair_g, x_u, send_o)
    pair_u = over_pair(x_u)
    got_o = over_core(send_o)
    d, g = order(lambda d, line, g, pair: (add(d, line), add(g, pair)), d, line_d, g, pair_g)
    mid_d, line_g = send(d, across), send(g, inward)
    send_k, keep_k = order(kv_pieces, n1, qgrad, kgrad, vgrad)
    x_o, o = order(first, keep_o, got_o)
    pair_u, x_o, send_k = order(same, pair_u, x_o, send_k)
    pair_o = over_pair(x_o)
    got_k = over_core(send_k)

    def layer(middle, part, got):
        return (mine(middle) + (mine(part).astype(F32) + got.astype(F32))).astype(BF16)

    layer_out = order(layer, middle, mlp_part, mlp_got)

    def turn(kept, line, inner, mid, new, pair):
        inner = add(inner, mid)
        new = add(new, pair)
        return jnp.where(edge, new, inner), add(kept, line), inner, new

    step, g, d, u = order(turn, g, line_g, d, mid_d, u, pair_u)
    line_du, mid_g = send(step, between), send(g, across)
    arrived = over_tensor(n1g)
    x_k, k = order(first, keep_k, got_k)
    pair_o, x_k = order(same, pair_o, x_k)
    pair_k = over_pair(x_k)

    def z(out, line, new, inner, mid, newest, pair):
        inner = add(inner, mid)
        newest = add(newest, pair)
        return jnp.where(edge, newest, inner), add(new, line), jnp.where(edge, line, out), inner, newest

    step, u, d, g, o = order(z, d, line_du, u, g, mid_g, o, pair_o)
    line_go, mid_u = send(step, between), send(u, across)
    pair_k, d = order(same, pair_k, d)
    near_d = over_pair(d)
    input_grad, gains = order(ending, n1g, arrived, mgrad, mgg)

    def z_last(out, line, new, inner, mid, newest, pair, gains):
        inner = add(inner, mid)
        newest = jnp.concatenate([add(newest, pair), jnp.pad(gains, ((0, 13), (0, 0))).astype(BF16)], 0)
        step = jnp.where(edge, newest, jnp.pad(inner, ((0, 16), (0, 0))))
        return step, add(new, line), jnp.where(edge, line, out), inner, newest

    step, o, g, u, k = order(z_last, g, line_go, o, u, mid_u, k, pair_k, gains)
    line_uk, mid_o = send(step, between), send(o, across)
    near_d, g = order(same, near_d, g)
    near_g = over_pair(g)
    far_d, far_near_d = over_core(d), over_core(near_d)
    u, k, o = order(lambda u, line, k, o, mid: (jnp.where(edge, line[: high + low], u), add(k, line), add(o, mid)),
                    u, line_uk, k, o, mid_o)
    line_o, mid_k = send(o, outward), send(k, across)
    near_g, u = order(same, near_g, u)
    near_u = over_pair(u)
    far_g, far_near_g = over_core(g), over_core(near_g)
    (down_wgrad,) = order(lambda *a: place(ids, 0, a, down_outs, "down_place"), d, near_d, far_d, far_near_d)
    o, k = order(lambda o, line, k, mid: (jnp.where(edge, line, o), add(k, mid)), o, line_o, k, mid_k)
    line_k = send(k, outward)
    near_u, o = order(same, near_u, o)
    near_o = over_pair(o)
    far_u, far_near_u = over_core(u), over_core(near_u)
    (gate_wgrad,) = order(lambda *a: place(ids, 0, a, hidden_outs, "gate_place"), g, near_g, far_g, far_near_g)
    k = order(lambda k, line: jnp.where(edge, line, k), k, line_k)
    near_o, k = order(same, near_o, k)
    near_k = over_pair(k)
    far_o, far_near_o, far_k = over_core(o), over_core(near_o), over_core(k)
    (up_wgrad,) = order(lambda *a: place(ids, 0, a, hidden_outs, "up_place"), u, near_u, far_u, far_near_u)
    out_wgrad, query_wgrad = order(
        lambda *a: place(
            ids, 0, a, [(high, width, 0, width, ((0, high, 1, 0, width, 0),)),
                        (high, thin, 0, wide, ((high, high, 2, 0, thin, 0),))], "out_query_place"),
        o, near_o, far_o, far_near_o)
    last_outs = [
        (high, thin, 0, thin, ((0, high, 1, 0, thin, 0),)), (high, thin, 0, thin, ((0, high, 1, thin, thin, 0),)),
        (high, thin, 1, wide, ((high, high, 2, 0, thin, 0),)), (16, width, 0, width, ((high + low, 16, 1, 0, width, 0),))]
    key_wgrad, value_wgrad, query_wgrad, gains = order(
        lambda k, q: place(ids, 0, [k], last_outs, "own_place", [None, None, q, None]), k, query_wgrad)
    (near_k,) = order(lambda a: (a,), near_k)
    far_near_k = over_core(near_k)
    key_wgrad, value_wgrad, query_wgrad, gains = order(
        lambda a, b, *e: place(ids, 1, [a, b], last_outs, "beside_place", e), near_k, far_k, key_wgrad, value_wgrad,
        query_wgrad, gains)
    key_wgrad, value_wgrad, query_wgrad, gains = order(
        lambda a, *e: place(ids, 3, [a], last_outs, "far_place", e), far_near_k, key_wgrad, value_wgrad, query_wgrad, gains)
    gains = gains.reshape(4, 16, width).sum(0)
    return (
        layer_out, input_grad, gains[0], query_wgrad, key_wgrad, value_wgrad,
        gains[2, :HEAD_SIZE], gains[2, HEAD_SIZE : 2 * HEAD_SIZE], out_wgrad,
        gains[1], gate_wgrad, up_wgrad, down_wgrad,
    )


def solution(mesh):
    rows, cols, rep = P("tensor", None), P(None, "tensor"), P()
    both = P("dp", "tensor")
    return jax.shard_map(
        functools.partial(per_device, mesh.shape["dp"], mesh.shape["tensor"]),
        mesh=mesh,
        in_specs=(both, both, rep, cols, cols, cols, rep, rep, rows, rep, cols, cols, rows),
        out_specs=(both, both, rep, cols, cols, cols, rep, rep, rows, rep, cols, cols, rows),
        check_vma=False,
    )
```

```python
import functools

import jax
import jax.numpy as jnp
import numpy as np
from jax import lax
from jax.experimental import pallas as pl
from jax.experimental.pallas import tpu as pltpu
from jax.sharding import PartitionSpec as P

HEAD_SIZE = 128
SEQUENCE_LENGTH = 384
epsilon = 1e-06
rope_base = 1000000.0
F32 = jnp.float32
BF16 = jnp.bfloat16
def dot_nn(a, b):
    return lax.dot_general(a, b, (((1,), (0,)), ((), ())), preferred_element_type=F32)


def dot_nt(a, b):
    return lax.dot_general(a, b, (((1,), (1,)), ((), ())), preferred_element_type=F32)


def dot_tn(a, b):
    return lax.dot_general(a, b, (((0,), (0,)), ((), ())), preferred_element_type=F32)


def rope_tables():
    half = HEAD_SIZE // 2
    frequency = rope_base ** (-np.arange(half, dtype=np.float64) * (2.0 / HEAD_SIZE))
    angle = np.arange(SEQUENCE_LENGTH, dtype=np.float64)[:, None] * frequency[None, :]
    cosine, sine = np.cos(angle), np.sin(angle)
    return (
        np.concatenate([cosine, cosine], 1).astype(np.float32),
        np.concatenate([-sine, sine], 1).astype(np.float32),
    )


def inv_rms(v):
    return lax.rsqrt(jnp.mean(v * v, -1, keepdims=True) + epsilon)


def near(x):
    return pltpu.with_memory_space_constraint(x, pltpu.VMEM)


def call(kernel, outs, name, *args, anywhere=(), far_outs=(), megabytes=14, **more):
    place = lambda a: a if a.dtype == jnp.int32 else near(a)
    return pl.pallas_call(
        kernel,
        in_specs=[pl.BlockSpec(memory_space=pltpu.SMEM if a.dtype == jnp.int32 else pltpu.VMEM) for a in args]
        + [pl.BlockSpec(memory_space=pltpu.HBM) for _ in anywhere],
        out_specs=[pl.BlockSpec(memory_space=pltpu.VMEM) for _ in outs]
        + [pl.BlockSpec(memory_space=pltpu.HBM) for _ in far_outs],
        out_shape=[pltpu.VMEM(shape, kind) for shape, kind in outs]
        + [pltpu.HBM(shape, kind) for shape, kind in far_outs],
        compiler_params=pltpu.CompilerParams(vmem_limit_bytes=megabytes * 1024 * 1024),
        name=name,
        **more,
    )(*(place(a) for a in args), *(pltpu.with_memory_space_constraint(a, pltpu.HBM) for a in anywhere))


def fetch(sources, targets, sem):
    copies = [pltpu.make_async_copy(s, t, sem.at[i]) for i, (s, t) in enumerate(zip(sources, targets))]
    for copy in copies:
        copy.start()
    return copies


def join(side, ins, out_ref, sem):
    if len(ins) == 1:
        return [pltpu.make_async_copy(ins[0], out_ref, sem.at[0])]
    share = ins[0].shape[1]
    places = [pl.ds(pl.multiple_of(half * share, share), share) for half in (side, 1 - side)]
    return [pltpu.make_async_copy(ref, out_ref.at[:, at], sem.at[i]) for i, (ref, at) in enumerate(zip(ins, places))]


def attn_fwd_kernel(
    n, ids_ref, gains_ref, *refs
):
    weights, table_hbm, refs = refs[n : n + 4], refs[n + 4], [*refs[:n], *refs[n + 5 :]]
    x_ref, branch_ref = refs[n : n + 2]
    outs, (n1_ref, qraw_ref, kraw_ref, qrot_ref, krot_ref, v_ref, p_ref, al_ref) = refs[n + 2 : n + 10], refs[n + 10 : n + 18]
    wq_ref, wkv_ref, wo_ref, table_ref, sem, weight_sem, out_sem, table_sem = refs[n + 18 :]
    scratch = (n1_ref, qraw_ref, kraw_ref, qrot_ref, krot_ref, v_ref, p_ref, al_ref)
    groups = wkv_ref.shape[0]
    heads = wq_ref.shape[2] // HEAD_SIZE
    written = [pltpu.make_async_copy(s, o, out_sem.at[i]) for i, (s, o) in enumerate(zip(scratch, outs))]
    written[3] = [pltpu.make_async_copy(qrot_ref.at[g], outs[3].at[g], out_sem.at[8 + 2 * g]) for g in range(groups)]
    written[6] = [pltpu.make_async_copy(p_ref.at[g], outs[6].at[g], out_sem.at[9 + 2 * g]) for g in range(groups)]
    copies = join(ids_ref[2], refs[:n], x_ref, sem)
    for copy in copies:
        copy.start()
    wq_hbm, wk_hbm, wv_hbm, wo_hbm = weights
    loads = []
    for g in range(groups):
        kv = slice(g * HEAD_SIZE, (g + 1) * HEAD_SIZE)
        pairs = ((wq_hbm.at[:, g * heads * HEAD_SIZE : (g + 1) * heads * HEAD_SIZE], wq_ref.at[g]),
                 (wk_hbm.at[:, kv], wkv_ref.at[g, :, :HEAD_SIZE]), (wv_hbm.at[:, kv], wkv_ref.at[g, :, HEAD_SIZE:]))
        loads.append([pltpu.make_async_copy(s, t, weight_sem.at[3 * g + i]) for i, (s, t) in enumerate(pairs)])
    load_out = pltpu.make_async_copy(wo_hbm, wo_ref, weight_sem.at[3 * groups])
    for copy in loads[0]:
        copy.start()
    tables = pltpu.make_async_copy(table_hbm, table_ref, table_sem)
    tables.start()
    gain, q_gain, k_gain = gains_ref[0:1, :], gains_ref[2:3, :HEAD_SIZE], gains_ref[2:3, HEAD_SIZE : 2 * HEAD_SIZE]
    for copy in copies:
        copy.wait()
    for copy in [c for group in loads[1:] for c in group]:
        copy.start()
    rows = x_ref.shape[0]
    x = x_ref[...].astype(F32)
    n1 = (x * inv_rms(x) * gain).astype(BF16)
    n1_ref[...] = n1
    tables.wait()
    cosine, sine = table_ref[:rows, :], table_ref[rows:, :]

    def rotate(raw, gain):
        n = raw * inv_rms(raw) * gain
        return n * cosine + pltpu.roll(n, HEAD_SIZE // 2, 1) * sine

    scale = HEAD_SIZE ** (-0.5)
    allowed = lax.broadcasted_iota(jnp.int32, (rows, rows), 1) <= lax.broadcasted_iota(jnp.int32, (rows, rows), 0)
    for g in range(groups):
        kv = slice(g * HEAD_SIZE, (g + 1) * HEAD_SIZE)
        for copy in loads[g]:
            copy.wait()
        q_raw = dot_nn(n1, wq_ref[g])
        kv_raw = dot_nn(n1, wkv_ref[g])
        k_raw, v = kv_raw[:, :HEAD_SIZE], kv_raw[:, HEAD_SIZE:].astype(BF16)
        qraw_ref[:, g * heads * HEAD_SIZE : (g + 1) * heads * HEAD_SIZE] = q_raw.astype(BF16)
        kraw_ref[:, kv] = k_raw.astype(BF16)
        v_ref[:, kv] = v
        k_rot = rotate(k_raw, k_gain).astype(BF16)
        krot_ref[:, kv] = k_rot
        for h in range(heads):
            at = slice((g * heads + h) * HEAD_SIZE, (g * heads + h + 1) * HEAD_SIZE)
            here = slice(h * rows, (h + 1) * rows)
            q_rot = (rotate(q_raw[:, h * HEAD_SIZE : (h + 1) * HEAD_SIZE], q_gain) * scale).astype(BF16)
            qrot_ref[g, here, :] = q_rot
            scores = jnp.where(allowed, dot_nt(q_rot, k_rot), -1e30)
            raised = jnp.exp(scores - jnp.max(scores, -1, keepdims=True))
            prob = (raised * (1.0 / jnp.sum(raised, -1, keepdims=True))).astype(BF16)
            p_ref[g, here, :] = prob
            al_ref[:, at] = dot_nn(prob, v).astype(BF16)
        written[3][g].start()
        written[6][g].start()
        if g == 0:
            written[0].start()
            load_out.start()
    for i in (1, 2, 4, 5, 7):
        written[i].start()
    load_out.wait()
    branch_ref[...] = dot_nn(al_ref[...], wo_ref[...]).astype(BF16)
    for copy in jax.tree.leaves(written, is_leaf=lambda c: not isinstance(c, list)):
        copy.wait()


def attn_fwd(ids, xs, gains, wq, wk, wv, wo, tables):
    rows, width = xs[0].shape[0], wq.shape[0]
    groups = wk.shape[1] // HEAD_SIZE
    heads = wq.shape[1] // wk.shape[1]
    full, kv, q = (rows, width), (rows, wk.shape[1]), (rows, wq.shape[1])
    far_outs = [(full, BF16), (q, BF16), (kv, BF16), ((groups, heads * rows, HEAD_SIZE), BF16), (kv, BF16), (kv, BF16),
                ((groups, heads * rows, rows), BF16), (q, BF16)]
    return call(
        functools.partial(attn_fwd_kernel, len(xs)), [(full, BF16), (full, BF16)], "attention_forward",
        ids, gains, anywhere=(*xs, wq, wk, wv, wo, tables), far_outs=far_outs,
        megabytes=32,
        scratch_shapes=[pltpu.VMEM(*o) for o in far_outs] + [
            pltpu.VMEM((groups, width, heads * HEAD_SIZE), BF16), pltpu.VMEM((groups, width, 2 * HEAD_SIZE), BF16),
            pltpu.VMEM(wo.shape, BF16)]
        + [pltpu.VMEM(tables.shape, F32), pltpu.SemaphoreType.DMA((2,)), pltpu.SemaphoreType.DMA((3 * groups + 1,)),
           pltpu.SemaphoreType.DMA((8 + 2 * groups,)), pltpu.SemaphoreType.DMA],
    )


def mlp_kernel(n, ids_ref, x_ref, own_ref, other_ref, gains_ref, wg_ref, wu_ref, wd_ref, *refs):
    cot_ref, mid_ref, n2_ref, hid_ref, gg_ref, ug_ref, out_ref, ngrad_ref, sem = refs[n:]
    copies = join(ids_ref[2], refs[:n], cot_ref, sem)
    for copy in copies:
        copy.start()
    units = wg_ref.shape[1]
    step = 512 if units % 512 == 0 else units
    middle = x_ref[...].astype(F32) + (own_ref[...].astype(F32) + other_ref[...].astype(F32))
    mid_ref[...] = middle
    n2 = (middle * inv_rms(middle) * gains_ref[1:2, :]).astype(BF16)
    n2_ref[...] = n2
    for copy in copies:
        copy.wait()
    for j in range(0, units, step):
        at = slice(j, j + step)
        gate = dot_nn(n2, wg_ref[:, at])
        up = dot_nn(n2, wu_ref[:, at])
        hgrad = dot_nt(cot_ref[...], wd_ref[at, :])
        sig = jax.nn.sigmoid(gate)
        silu = gate * sig
        hid_ref[:, at] = (silu * up).astype(BF16)
        gg_ref[:, at] = (hgrad * up * sig * (1.0 + gate * (1.0 - sig))).astype(BF16)
        ug_ref[:, at] = (hgrad * silu).astype(BF16)
    ngrad_ref[...] = (dot_nt(gg_ref[...], wg_ref[...]) + dot_nt(ug_ref[...], wu_ref[...])).astype(BF16)
    out_ref[...] = dot_nn(hid_ref[...], wd_ref[...]).astype(BF16)


def mlp(ids, x, own, other, gains, wg, wu, wd, cots):
    full, hid = x.shape, (x.shape[0], wg.shape[1])
    outs = [(full, F32), (full, BF16), (hid, BF16), (hid, BF16), (hid, BF16), (full, BF16), (full, BF16)]
    return call(
        functools.partial(mlp_kernel, len(cots)), [(full, BF16)] + outs, "feed_forward",
        ids, x, own, other, gains, wg, wu, wd, anywhere=cots, scratch_shapes=[pltpu.SemaphoreType.DMA((2,))],
    )


def quarter(r, ids):
    core = 1 - ids[0] if r < 2 else ids[0]
    return 2 * core + (1 - ids[1] if r % 2 == 0 else ids[1])


def pieces_kernel(layouts, ids_ref, *refs):
    n = sum(len(layout) for _, layout in layouts)
    ins, outs = refs[: 2 * n], refs[2 * n :]
    i = 0
    for (base, layout), out_ref in zip(layouts, outs):
        for wide, begin, row, fold, lane in layout:
            a_ref, b_ref = ins[2 * i], ins[2 * i + 1]
            i += 1
            size = a_ref.shape[1] // 4
            for r in range(2):
                at = pl.multiple_of(quarter(base + r, ids_ref) * size, size)
                w = dot_tn(a_ref[:, pl.ds(at, size)], b_ref[:, begin : begin + wide]).astype(BF16)
                high = size // fold
                for f in range(fold):
                    lanes = slice(lane + f * wide, lane + (f + 1) * wide)
                    out_ref[r, row : row + high, lanes] = w[f * high : (f + 1) * high]


def pieces(ids, chunks, name):
    layouts = tuple((base, tuple(part[2:] for part in parts)) for base, parts, _, _ in chunks)
    args = [x for _, parts, _, _ in chunks for part in parts for x in part[:2]]
    outs = [((2, rows, width), BF16) for _, _, rows, width in chunks]
    return call(functools.partial(pieces_kernel, layouts), outs, name, ids, *args)


def place_kernel(layout, n, ids_ref, *refs):
    outs = refs[-len(layout) :]
    i = pl.program_id(0)

    def spread(piece):
        for out_ref, segments in zip(outs, layout):
            for row, high, fold, lane, wide, to in segments:
                h = high // fold
                for f in range(fold):
                    lanes = slice(lane + f * wide, lane + (f + 1) * wide)
                    out_ref[f * h : (f + 1) * h, to : to + wide] = piece[row : row + h, lanes].astype(F32)

    for k in range(n):
        pl.when(i == k)(functools.partial(lambda ref: spread(ref[...]), refs[k]))


def home(numbers, i, ids):
    r = sum(number * (i == k) for k, number in enumerate(numbers))
    core = jnp.where(r < 2, ids[0], 1 - ids[0])
    return 2 * core + jnp.where(r % 2 == 0, ids[1], 1 - ids[1])


def place(ids, numbers, sources, outs, name, earlier=None):
    earlier = earlier or [None] * len(outs)
    extra = [e for e in earlier if e is not None]
    n = len(sources)
    to = [k for k, e in enumerate(earlier) if e is not None]
    return pl.pallas_call(
        functools.partial(place_kernel, tuple(o[4] for o in outs), n),
        grid_spec=pltpu.PrefetchScalarGridSpec(
            num_scalar_prefetch=1,
            grid=(n,),
            in_specs=[pl.BlockSpec(memory_space=pltpu.VMEM)] * n + [pl.BlockSpec(memory_space=pl.ANY)] * len(extra),
            out_specs=[
                pl.BlockSpec((o[0], o[1]), functools.partial(lambda k, i, ids: (home(numbers, i, ids), k), o[2])) for o in outs
            ],
        ),
        out_shape=[jax.ShapeDtypeStruct((4 * o[0], o[3]), F32) for o in outs],
        input_output_aliases={1 + n + e: k for e, k in enumerate(to)},
        compiler_params=pltpu.CompilerParams(dimension_semantics=("arbitrary",), vmem_limit_bytes=24 * 1024 * 1024),
        name=name,
    )(ids, *(near(s) for s in sources), *extra)


def attn_bwd_kernel(heads, gains_ref, nother_ref, *refs):
    n = 14
    outs = refs[n : n + 7]
    bufs, (sem,) = refs[n + 7 : n + 7 + n], refs[n + 7 + n :]
    copies = [pltpu.make_async_copy(s, t, sem.at[i]) for i, (s, t) in enumerate(zip(refs[:n], bufs))]
    nown_ref, mid_ref, cot_ref, wo_ref, table_ref, v_ref, p_ref, krot_ref, qrot_ref, qraw_ref, kraw_ref = bufs[:11]
    wq_ref, wk_ref, wv_ref = bufs[11:]
    mgrad_ref, mgg_ref, blow_ref, qgrad_ref, kgrad_ref, vgrad_ref, n1g_ref = outs
    rows = kraw_ref.shape[0]
    groups = wk_ref.shape[1] // HEAD_SIZE
    q_gain, k_gain = gains_ref[2:3, :HEAD_SIZE], gains_ref[2:3, HEAD_SIZE : 2 * HEAD_SIZE]
    for copy in copies[:4]:
        copy.start()
    for copy in copies[:3]:
        copy.wait()
    for copy in copies[4:7]:
        copy.start()
    ngrad = nown_ref[...].astype(F32) + nother_ref[...].astype(F32)
    middle = mid_ref[...]
    inv = inv_rms(middle)
    u = middle * inv
    mgg_ref[...] = jnp.sum(ngrad * u, 0, keepdims=True)
    s = ngrad * gains_ref[1:2, :]
    mgrad = cot_ref[...].astype(F32) + inv * (s - u * jnp.mean(s * u, -1, keepdims=True))
    mgrad_ref[...] = mgrad
    blow_ref[...] = mgrad.astype(BF16)
    for copy in copies[7:]:
        copy.start()
    scale = HEAD_SIZE ** (-0.5)
    copies[3].wait()
    copies[4].wait()
    cosine, sine = table_ref[:rows, :], table_ref[rows:, :]
    agrads = dot_nt(blow_ref[...], wo_ref[...]).astype(BF16)

    def back(raw, gain, grad):
        inv = inv_rms(raw)
        u = raw * inv
        dn = grad * cosine + pltpu.roll(grad * sine, HEAD_SIZE // 2, 1)
        s = dn * gain
        return (
            (inv * (s - u * jnp.mean(s * u, -1, keepdims=True))).astype(BF16),
            jnp.sum(dn * u, 0, keepdims=True),
        )

    qgg = jnp.zeros((1, HEAD_SIZE), F32)
    kgg = jnp.zeros((1, HEAD_SIZE), F32)
    for copy in copies[5:11]:
        copy.wait()
    for g in range(groups):
        kv = slice(g * HEAD_SIZE, (g + 1) * HEAD_SIZE)
        krgrad, vgrad = 0.0, 0.0
        for h in range(heads):
            here = slice(h * rows, (h + 1) * rows)
            at = slice((g * heads + h) * HEAD_SIZE, (g * heads + h + 1) * HEAD_SIZE)
            agrad = agrads[:, at]
            prob = p_ref[g, here, :]
            prob_wide = prob.astype(F32)
            pgrad = dot_nt(agrad, v_ref[:, kv])
            sgrad = (prob_wide * (pgrad - jnp.sum(pgrad * prob_wide, -1, keepdims=True))).astype(BF16)
            vgrad += dot_tn(prob, agrad)
            krgrad += dot_tn(sgrad, qrot_ref[g, here, :])
            qgrad, part = back(qraw_ref[:, at].astype(F32), q_gain, dot_nn(sgrad, krot_ref[:, kv]) * scale)
            qgrad_ref[:, at] = qgrad
            qgg += part
        kgrad, part = back(kraw_ref[:, kv].astype(F32), k_gain, krgrad)
        kgrad_ref[:, kv] = kgrad
        vgrad_ref[:, kv] = vgrad.astype(BF16)
        kgg += part
    for copy in copies[11:]:
        copy.wait()
    total = (
        dot_nt(qgrad_ref[...], wq_ref[...]) + dot_nt(kgrad_ref[...], wk_ref[...]) + dot_nt(vgrad_ref[...], wv_ref[...])
    )
    width = total.shape[1]
    gains = jnp.concatenate([qgg, kgg, jnp.zeros((1, width - 2 * HEAD_SIZE), F32)], 1)
    gains = jnp.concatenate([gains, jnp.zeros((15, width), F32)], 0)
    n1g_ref[:rows] = total.astype(BF16)
    n1g_ref[rows:] = gains.astype(BF16)


def attn_bwd(nown, nother, middle, cot, gains, weights, prob, qraw, kraw, qrot, krot, v, tables):
    wq, wk, wv, wo = weights
    rows, width = middle.shape
    full = (rows, width)
    outs = [(full, F32), ((1, width), F32), (full, BF16), (qraw.shape, BF16), (kraw.shape, BF16), (kraw.shape, BF16),
            ((rows + 16, width), BF16)]
    streams = (nown, middle, cot, wo, tables, v, prob, krot, qrot, qraw, kraw, wq, wk, wv)
    return call(
        functools.partial(attn_bwd_kernel, wq.shape[1] // wk.shape[1]), outs, "attention_backward",
        gains, nother, anywhere=streams, megabytes=36,
        scratch_shapes=[pltpu.VMEM(a.shape, a.dtype) for a in streams] + [pltpu.SemaphoreType.DMA((len(streams),))],
    )


def swap_pairs(n, bit):
    return [(i, i ^ bit) for i in range(n)]


def line_hops(n):
    step = n // 4
    shift = lambda a, b: [(a * step + r, b * step + r) for r in range(step)]
    return shift(0, 1) + shift(3, 2), shift(1, 2) + shift(2, 1), shift(1, 0) + shift(2, 3)


def add(a, b):
    return (a.astype(F32) + b.astype(F32)).astype(BF16)


def others(x, tensor):
    if tensor == 2:
        return lax.ppermute(x, "tensor", swap_pairs(2, 1))
    return (lax.psum(x.astype(F32), "tensor") - x.astype(F32)).astype(x.dtype)


def features(x, tensor):
    if tensor == 2:
        return x, lax.ppermute(x, "tensor", swap_pairs(2, 1))
    return (lax.all_gather(x, "tensor", axis=1, tiled=True),)


class Order:
    def __init__(self):
        self.last = None

    def __call__(self, step, *inputs):
        if self.last is not None:
            inputs, _ = lax.optimization_barrier((inputs, self.last))
        out = step(*inputs)
        self.last = jax.tree.leaves(out)
        return out


def per_device(
    dp, tensor, tokens, cotangent, attn_gain, query_weight, key_matrix, value_matrix, query_gain,
    key_norm_gain, out_weight, mlp_gain, gate_weight, up_weight, down_weight,
):
    rows, share = tokens.shape
    width = query_weight.shape[0]
    groups = key_matrix.shape[1] // HEAD_SIZE
    side = lax.axis_index("tensor")
    offset = side * share
    mine = lambda a: lax.dynamic_slice_in_dim(a, offset, share, 1)
    where = lax.axis_index("dp")
    core, pair, spot = where % 2, (where // 2) % 2, where // 4
    ids = jnp.stack([core, pair, side]).astype(jnp.int32)
    tables = jnp.asarray(np.concatenate(rope_tables(), 0))
    attn_gain = attn_gain[None]
    heads_gain = jnp.concatenate([query_gain, key_norm_gain, jnp.zeros((width - 2 * HEAD_SIZE,), F32)])[None]
    gains = jnp.concatenate([attn_gain, mlp_gain[None], heads_gain, jnp.zeros((5, width), F32)], 0)

    order = Order()
    xs = features(tokens, tensor)
    *xs, gains = order(lambda *a: a, *xs, order(lambda a: (a,), gains)[0])
    cots = features(order(lambda a: (a,), cotangent)[0], tensor)
    x, branch, n1, qraw, kraw, qrot, krot, v, prob, al = order(
        lambda *a: attn_fwd(ids, a, gains, query_weight, key_matrix, value_matrix, out_weight, tables), *xs)
    *cots, branch = order(lambda *a: a, *cots, branch)
    branch_got = others(branch, tensor)
    cot, middle, n2, hidden, ggrad, ugrad, mlp_part, ngrad = order(
        lambda own, other, *c: mlp(ids, x, own, other, gains, gate_weight, up_weight, down_weight, c),
        branch, branch_got, *cots)
    weights = (query_weight, key_matrix, value_matrix, out_weight)
    common = (gains, weights, prob, qraw, kraw, qrot, krot, v, tables)

    def ending(n1g, arrived, mgrad, mgg):
        n1_grad = n1g[:rows].astype(F32) + arrived[:rows].astype(F32)
        heads = n1g[rows : rows + 1].astype(F32) + arrived[rows : rows + 1].astype(F32)
        wide = x.astype(F32)
        inv_one = inv_rms(wide)
        u = wide * inv_one
        s = n1_grad * attn_gain
        mean = jnp.mean(s * u, -1, keepdims=True)
        input_grad = (mine(mgrad) + inv_one * (mine(s) - mine(u) * mean)).astype(BF16)
        return input_grad, jnp.concatenate([jnp.sum(n1_grad * u, 0, keepdims=True), mgg, heads], 0)

    if tensor != 2 or dp != 16:
        mgrad, mgg, blow, qgrad, kgrad, vgrad, n1g = attn_bwd(
            ngrad, others(ngrad, tensor), middle, cot, *common)
        input_grad, gains = ending(n1g, others(n1g, tensor), mgrad, mgg)
        total = lambda a: lax.psum(a.astype(BF16), "dp").astype(F32)
        agg, mgg, heads = total(lax.pmean(gains, "tensor"))
        layer_out = (mine(middle) + lax.psum_scatter(mlp_part, "tensor", scatter_dimension=1, tiled=True)).astype(BF16)
        return (
            layer_out, input_grad, agg, total(dot_tn(n1, qgrad)), total(dot_tn(n1, kgrad)), total(dot_tn(n1, vgrad)),
            heads[:HEAD_SIZE], heads[HEAD_SIZE : 2 * HEAD_SIZE], total(dot_tn(al, blow)), mgg,
            total(dot_tn(n2, ggrad)), total(dot_tn(n2, ugrad)), total(dot_tn(hidden, cot)),
        )

    edge = (spot == 0) | (spot == 3)
    inward, across, outward = line_hops(dp)
    between = inward + outward
    send = lambda x, hops: lax.ppermute(x, "dp", hops)
    over_core = lambda x: send(x, swap_pairs(dp, 1))
    over_pair = lambda x: send(x, swap_pairs(dp, 2))
    over_tensor = lambda x: lax.ppermute(x, "tensor", swap_pairs(2, 1))
    half = lambda a, b: lax.dynamic_slice_in_dim(a, b * share, share, 1)
    first = lambda keep, got: (add(keep[0], got[0]), add(keep[1], got[1]))
    same = lambda *a: a

    units, wide = gate_weight.shape[1], qraw.shape[1]
    high, low, thin = width // 4, width // 8, wide // 2
    size = hidden.shape[1] // 4
    rest = units - width

    def hidden_parts(a, b):
        return [(a, b, width, 0, 0, 1, 0), (a, b, rest, width, high, 2, 0)]

    hidden_outs = [(high, units, 0, units, ((0, high, 1, 0, width, 0), (high, high, 2, 0, rest, width)))]
    down_outs = [(size, width, 0, width, ((0, size, 1, 0, width, 0),))]

    nother = over_tensor(ngrad)
    send_d, keep_d = order(lambda h, c: pieces(ids, [(base, [(h, c, width, 0, 0, 1, 0)], size, width) for base in (0, 2)],
                                               "down_gradient"), hidden, cot)
    got_d = over_core(send_d)
    send_g, send_u = order(
        lambda n2, g, u: pieces(ids, [(0, hidden_parts(n2, g), size, width), (0, hidden_parts(n2, u), size, width)],
                                "gate_up_gradient_sent"), n2, ggrad, ugrad)
    x_d, d = order(first, keep_d, got_d)
    pair_d = over_pair(x_d)
    got_g, got_u = over_core(send_g), over_core(send_u)
    keep_g, keep_u = order(
        lambda n2, g, u: pieces(ids, [(2, hidden_parts(n2, g), size, width), (2, hidden_parts(n2, u), size, width)],
                                "gate_up_gradient_kept"), n2, ggrad, ugrad)
    x_g, g, x_u, u = order(lambda a, b, c, d: (*first(a, b), *first(c, d)), keep_g, got_g, keep_u, got_u)
    pair_d, nother, x_g = order(same, pair_d, nother, x_g)
    pair_g = over_pair(x_g)
    d, mlp_half = order(lambda a, b, m: (add(a, b), half(m, 1 - side)), d, pair_d, mlp_part)
    line_d, mlp_got = send(d, inward), over_tensor(mlp_half)
    mgrad, mgg, blow, qgrad, kgrad, vgrad, n1g = order(
        lambda *a: attn_bwd(*a, *common), ngrad, nother, middle, cot)

    def out_pieces(al, blow, n1, qgrad):
        parts = [(al, blow, width, 0, 0, 1, 0), (n1, qgrad, thin, 0, high, 2, 0)]
        return pieces(ids, [(base, parts, high + low, width) for base in (0, 2)], "out_query_gradient")

    def kv_pieces(n1, qgrad, kgrad, vgrad):
        parts = [(n1, kgrad, thin, 0, 0, 1, 0), (n1, vgrad, thin, 0, 0, 1, thin), (n1, qgrad, thin, thin, high, 2, 0)]
        return pieces(ids, [(base, parts, high + low, width) for base in (0, 2)], "key_value_query_gradient")

    send_o, keep_o = order(out_pieces, al, blow, n1, qgrad)
    line_d, pair_g, x_u, send_o = order(same, line_d, pair_g, x_u, send_o)
    pair_u = over_pair(x_u)
    got_o = over_core(send_o)
    d, g = order(lambda d, line, g, pair: (add(d, line), add(g, pair)), d, line_d, g, pair_g)
    mid_d, line_g = send(d, across), send(g, inward)
    send_k, keep_k = order(kv_pieces, n1, qgrad, kgrad, vgrad)
    x_o, o = order(first, keep_o, got_o)
    pair_u, x_o, send_k = order(same, pair_u, x_o, send_k)
    pair_o = over_pair(x_o)
    got_k = over_core(send_k)

    def layer(middle, part, got):
        return (mine(middle) + (mine(part).astype(F32) + got.astype(F32))).astype(BF16)

    layer_out = order(layer, middle, mlp_part, mlp_got)

    def turn(kept, line, inner, mid, new, pair):
        inner = add(inner, mid)
        new = add(new, pair)
        return jnp.where(edge, new, inner), add(kept, line), inner, new

    step, g, d, u = order(turn, g, line_g, d, mid_d, u, pair_u)
    line_du, mid_g = send(step, between), send(g, across)
    arrived = over_tensor(n1g)
    x_k, k = order(first, keep_k, got_k)
    pair_o, x_k = order(same, pair_o, x_k)
    pair_k = over_pair(x_k)

    def z(out, line, new, inner, mid, newest, pair):
        inner = add(inner, mid)
        newest = add(newest, pair)
        return jnp.where(edge, newest, inner), add(new, line), jnp.where(edge, line, out), inner, newest

    step, u, d, g, o = order(z, d, line_du, u, g, mid_g, o, pair_o)
    line_go, mid_u = send(step, between), send(u, across)
    pair_k, d = order(same, pair_k, d)
    near_d = over_pair(d)
    input_grad, gains = order(ending, n1g, arrived, mgrad, mgg)

    def z_last(out, line, new, inner, mid, newest, pair, gains):
        inner = add(inner, mid)
        newest = jnp.concatenate([add(newest, pair), jnp.pad(gains, ((0, 13), (0, 0))).astype(BF16)], 0)
        step = jnp.where(edge, newest, jnp.pad(inner, ((0, 16), (0, 0))))
        return step, add(new, line), jnp.where(edge, line, out), inner, newest

    step, o, g, u, k = order(z_last, g, line_go, o, u, mid_u, k, pair_k, gains)
    line_uk, mid_o = send(step, between), send(o, across)
    near_d, g = order(same, near_d, g)
    near_g = over_pair(g)
    far_d, far_near_d = over_core(d), over_core(near_d)
    u, k, o = order(lambda u, line, k, o, mid: (jnp.where(edge, line[: high + low], u), add(k, line), add(o, mid)),
                    u, line_uk, k, o, mid_o)
    line_o, mid_k = send(o, outward), send(k, across)
    near_g, u = order(same, near_g, u)
    near_u = over_pair(u)
    far_g, far_near_g = over_core(g), over_core(near_g)
    (down_wgrad,) = order(lambda *a: place(ids, (0, 1, 2, 3), a, down_outs, "down_place"), d, near_d, far_d, far_near_d)
    o, k = order(lambda o, line, k, mid: (jnp.where(edge, line, o), add(k, mid)), o, line_o, k, mid_k)
    line_k = send(k, outward)
    near_u, o = order(same, near_u, o)
    near_o = over_pair(o)
    far_u, far_near_u = over_core(u), over_core(near_u)
    (gate_wgrad,) = order(lambda *a: place(ids, (0, 1, 2, 3), a, hidden_outs, "gate_place"), g, near_g, far_g, far_near_g)
    k = order(lambda k, line: jnp.where(edge, line, k), k, line_k)
    near_o, k = order(same, near_o, k)
    near_k = over_pair(k)
    far_o, far_near_o, far_k = over_core(o), over_core(near_o), over_core(k)
    (up_wgrad,) = order(lambda *a: place(ids, (0, 1, 2, 3), a, hidden_outs, "up_place"), u, near_u, far_u, far_near_u)
    out_wgrad, query_wgrad = order(
        lambda *a: place(
            ids, (0, 1, 2, 3), a, [(high, width, 0, width, ((0, high, 1, 0, width, 0),)),
                        (high, thin, 0, wide, ((high, high, 2, 0, thin, 0),))], "out_query_place"),
        o, near_o, far_o, far_near_o)
    last_outs = [
        (high, thin, 0, thin, ((0, high, 1, 0, thin, 0),)), (high, thin, 0, thin, ((0, high, 1, thin, thin, 0),)),
        (high, thin, 1, wide, ((high, high, 2, 0, thin, 0),)), (16, width, 0, width, ((high + low, 16, 1, 0, width, 0),))]
    key_wgrad, value_wgrad, query_wgrad, gains = order(
        lambda k, far, q: place(ids, (0, 2), [k, far], last_outs, "own_place", [None, None, q, None]), k, far_k,
        query_wgrad)
    (near_k,) = order(lambda a: (a,), near_k)
    far_near_k = over_core(near_k)
    key_wgrad, value_wgrad, query_wgrad, gains = order(
        lambda a, *e: place(ids, (1,), [a], last_outs, "beside_place", e), near_k, key_wgrad, value_wgrad,
        query_wgrad, gains)
    key_wgrad, value_wgrad, query_wgrad, gains = order(
        lambda a, *e: place(ids, (3,), [a], last_outs, "far_place", e), far_near_k, key_wgrad, value_wgrad, query_wgrad, gains)
    gains = gains.reshape(4, 16, width).sum(0)
    return (
        layer_out, input_grad, gains[0], query_wgrad, key_wgrad, value_wgrad,
        gains[2, :HEAD_SIZE], gains[2, HEAD_SIZE : 2 * HEAD_SIZE], out_wgrad,
        gains[1], gate_wgrad, up_wgrad, down_wgrad,
    )


def solution(mesh):
    rows, cols, rep = P("tensor", None), P(None, "tensor"), P()
    both = P("dp", "tensor")
    return jax.shard_map(
        functools.partial(per_device, mesh.shape["dp"], mesh.shape["tensor"]),
        mesh=mesh,
        in_specs=(both, both, rep, cols, cols, cols, rep, rep, rows, rep, cols, cols, rows),
        out_specs=(both, both, rep, cols, cols, cols, rep, rep, rows, rep, cols, cols, rows),
        check_vma=False,
    )
```

```python
import functools

import jax
import jax.numpy as jnp
import numpy as np
from jax import lax
from jax.experimental import pallas as pl
from jax.experimental.pallas import tpu as pltpu
from jax.sharding import PartitionSpec as P

HEAD_SIZE = 128
SEQUENCE_LENGTH = 384
epsilon = 1e-06
rope_base = 1000000.0
F32 = jnp.float32
BF16 = jnp.bfloat16
def dot_nn(a, b):
    return lax.dot_general(a, b, (((1,), (0,)), ((), ())), preferred_element_type=F32)


def dot_nt(a, b):
    return lax.dot_general(a, b, (((1,), (1,)), ((), ())), preferred_element_type=F32)


def dot_tn(a, b):
    return lax.dot_general(a, b, (((0,), (0,)), ((), ())), preferred_element_type=F32)


def rope_tables():
    half = HEAD_SIZE // 2
    frequency = rope_base ** (-np.arange(half, dtype=np.float64) * (2.0 / HEAD_SIZE))
    angle = np.arange(SEQUENCE_LENGTH, dtype=np.float64)[:, None] * frequency[None, :]
    cosine, sine = np.cos(angle), np.sin(angle)
    return (
        np.concatenate([cosine, cosine], 1).astype(np.float32),
        np.concatenate([-sine, sine], 1).astype(np.float32),
    )


def inv_rms(v):
    return lax.rsqrt(jnp.mean(v * v, -1, keepdims=True) + epsilon)


def near(x):
    return pltpu.with_memory_space_constraint(x, pltpu.VMEM)


def call(kernel, outs, name, *args, anywhere=(), far_outs=(), megabytes=14, **more):
    place = lambda a: a if a.dtype == jnp.int32 else near(a)
    return pl.pallas_call(
        kernel,
        in_specs=[pl.BlockSpec(memory_space=pltpu.SMEM if a.dtype == jnp.int32 else pltpu.VMEM) for a in args]
        + [pl.BlockSpec(memory_space=pltpu.HBM) for _ in anywhere],
        out_specs=[pl.BlockSpec(memory_space=pltpu.VMEM) for _ in outs]
        + [pl.BlockSpec(memory_space=pltpu.HBM) for _ in far_outs],
        out_shape=[pltpu.VMEM(shape, kind) for shape, kind in outs]
        + [pltpu.HBM(shape, kind) for shape, kind in far_outs],
        compiler_params=pltpu.CompilerParams(vmem_limit_bytes=megabytes * 1024 * 1024),
        name=name,
        **more,
    )(*(place(a) for a in args), *(pltpu.with_memory_space_constraint(a, pltpu.HBM) for a in anywhere))


def fetch(sources, targets, sem):
    copies = [pltpu.make_async_copy(s, t, sem.at[i]) for i, (s, t) in enumerate(zip(sources, targets))]
    for copy in copies:
        copy.start()
    return copies


def join(side, ins, out_ref, sem):
    if len(ins) == 1:
        return [pltpu.make_async_copy(ins[0], out_ref, sem.at[0])]
    share = ins[0].shape[1]
    places = [pl.ds(pl.multiple_of(half * share, share), share) for half in (side, 1 - side)]
    return [pltpu.make_async_copy(ref, out_ref.at[:, at], sem.at[i]) for i, (ref, at) in enumerate(zip(ins, places))]


def attn_fwd_kernel(
    n, ids_ref, gains_ref, *refs
):
    weights, table_hbm, refs = refs[n : n + 4], refs[n + 4], [*refs[:n], *refs[n + 5 :]]
    x_ref, branch_ref = refs[n : n + 2]
    outs, (n1_ref, qraw_ref, kraw_ref, qrot_ref, krot_ref, v_ref, p_ref, al_ref) = refs[n + 2 : n + 10], refs[n + 10 : n + 18]
    wq_ref, wkv_ref, wo_ref, table_ref, sem, weight_sem, out_sem, table_sem = refs[n + 18 :]
    scratch = (n1_ref, qraw_ref, kraw_ref, qrot_ref, krot_ref, v_ref, p_ref, al_ref)
    groups = wkv_ref.shape[0]
    heads = wq_ref.shape[2] // HEAD_SIZE
    written = [pltpu.make_async_copy(s, o, out_sem.at[i]) for i, (s, o) in enumerate(zip(scratch, outs))]
    written[3] = [pltpu.make_async_copy(qrot_ref.at[g], outs[3].at[g], out_sem.at[8 + 2 * g]) for g in range(groups)]
    written[6] = [pltpu.make_async_copy(p_ref.at[g], outs[6].at[g], out_sem.at[9 + 2 * g]) for g in range(groups)]
    copies = join(ids_ref[2], refs[:n], x_ref, sem)
    for copy in copies:
        copy.start()
    wq_hbm, wk_hbm, wv_hbm, wo_hbm = weights
    loads = []
    for g in range(groups):
        kv = slice(g * HEAD_SIZE, (g + 1) * HEAD_SIZE)
        pairs = ((wq_hbm.at[:, g * heads * HEAD_SIZE : (g + 1) * heads * HEAD_SIZE], wq_ref.at[g]),
                 (wk_hbm.at[:, kv], wkv_ref.at[g, :, :HEAD_SIZE]), (wv_hbm.at[:, kv], wkv_ref.at[g, :, HEAD_SIZE:]))
        loads.append([pltpu.make_async_copy(s, t, weight_sem.at[3 * g + i]) for i, (s, t) in enumerate(pairs)])
    load_out = pltpu.make_async_copy(wo_hbm, wo_ref, weight_sem.at[3 * groups])
    for copy in loads[0]:
        copy.start()
    tables = pltpu.make_async_copy(table_hbm, table_ref, table_sem)
    tables.start()
    gain, q_gain, k_gain = gains_ref[0:1, :], gains_ref[2:3, :HEAD_SIZE], gains_ref[2:3, HEAD_SIZE : 2 * HEAD_SIZE]
    for copy in copies:
        copy.wait()
    for copy in [c for group in loads[1:] for c in group]:
        copy.start()
    rows = x_ref.shape[0]
    x = x_ref[...].astype(F32)
    n1 = (x * inv_rms(x) * gain).astype(BF16)
    n1_ref[...] = n1
    tables.wait()
    cosine, sine = table_ref[:rows, :], table_ref[rows:, :]

    def rotate(raw, gain):
        n = raw * inv_rms(raw) * gain
        return n * cosine + pltpu.roll(n, HEAD_SIZE // 2, 1) * sine

    scale = HEAD_SIZE ** (-0.5)
    allowed = lax.broadcasted_iota(jnp.int32, (rows, rows), 1) <= lax.broadcasted_iota(jnp.int32, (rows, rows), 0)
    for g in range(groups):
        kv = slice(g * HEAD_SIZE, (g + 1) * HEAD_SIZE)
        for copy in loads[g]:
            copy.wait()
        q_raw = dot_nn(n1, wq_ref[g])
        kv_raw = dot_nn(n1, wkv_ref[g])
        k_raw, v = kv_raw[:, :HEAD_SIZE], kv_raw[:, HEAD_SIZE:].astype(BF16)
        qraw_ref[:, g * heads * HEAD_SIZE : (g + 1) * heads * HEAD_SIZE] = q_raw.astype(BF16)
        kraw_ref[:, kv] = k_raw.astype(BF16)
        v_ref[:, kv] = v
        k_rot = rotate(k_raw, k_gain).astype(BF16)
        krot_ref[:, kv] = k_rot
        for h in range(heads):
            at = slice((g * heads + h) * HEAD_SIZE, (g * heads + h + 1) * HEAD_SIZE)
            here = slice(h * rows, (h + 1) * rows)
            q_rot = (rotate(q_raw[:, h * HEAD_SIZE : (h + 1) * HEAD_SIZE], q_gain) * scale).astype(BF16)
            qrot_ref[g, here, :] = q_rot
            scores = jnp.where(allowed, dot_nt(q_rot, k_rot), -1e30)
            raised = jnp.exp(scores - jnp.max(scores, -1, keepdims=True))
            prob = (raised * (1.0 / jnp.sum(raised, -1, keepdims=True))).astype(BF16)
            p_ref[g, here, :] = prob
            al_ref[:, at] = dot_nn(prob, v).astype(BF16)
        written[3][g].start()
        written[6][g].start()
        if g == 0:
            written[0].start()
            load_out.start()
    for i in (1, 2, 4, 5, 7):
        written[i].start()
    load_out.wait()
    branch_ref[...] = dot_nn(al_ref[...], wo_ref[...]).astype(BF16)
    for copy in jax.tree.leaves(written, is_leaf=lambda c: not isinstance(c, list)):
        copy.wait()


def attn_fwd(ids, xs, gains, wq, wk, wv, wo, tables):
    rows, width = xs[0].shape[0], wq.shape[0]
    groups = wk.shape[1] // HEAD_SIZE
    heads = wq.shape[1] // wk.shape[1]
    full, kv, q = (rows, width), (rows, wk.shape[1]), (rows, wq.shape[1])
    far_outs = [(full, BF16), (q, BF16), (kv, BF16), ((groups, heads * rows, HEAD_SIZE), BF16), (kv, BF16), (kv, BF16),
                ((groups, heads * rows, rows), BF16), (q, BF16)]
    return call(
        functools.partial(attn_fwd_kernel, len(xs)), [(full, BF16), (full, BF16)], "attention_forward",
        ids, gains, anywhere=(*xs, wq, wk, wv, wo, tables), far_outs=far_outs,
        megabytes=32,
        scratch_shapes=[pltpu.VMEM(*o) for o in far_outs] + [
            pltpu.VMEM((groups, width, heads * HEAD_SIZE), BF16), pltpu.VMEM((groups, width, 2 * HEAD_SIZE), BF16),
            pltpu.VMEM(wo.shape, BF16)]
        + [pltpu.VMEM(tables.shape, F32), pltpu.SemaphoreType.DMA((2,)), pltpu.SemaphoreType.DMA((3 * groups + 1,)),
           pltpu.SemaphoreType.DMA((8 + 2 * groups,)), pltpu.SemaphoreType.DMA],
    )


def mlp_kernel(n, ids_ref, x_ref, own_ref, other_ref, gains_ref, wg_ref, wu_ref, wd_ref, *refs):
    cot_ref, mid_ref, n2_ref, hid_ref, gg_ref, ug_ref, out_ref, ngrad_ref, sem = refs[n:]
    copies = join(ids_ref[2], refs[:n], cot_ref, sem)
    for copy in copies:
        copy.start()
    units = wg_ref.shape[1]
    step = 512 if units % 512 == 0 else units
    middle = x_ref[...].astype(F32) + (own_ref[...].astype(F32) + other_ref[...].astype(F32))
    mid_ref[...] = middle
    n2 = (middle * inv_rms(middle) * gains_ref[1:2, :]).astype(BF16)
    n2_ref[...] = n2
    for copy in copies:
        copy.wait()
    for j in range(0, units, step):
        at = slice(j, j + step)
        gate = dot_nn(n2, wg_ref[:, at])
        up = dot_nn(n2, wu_ref[:, at])
        hgrad = dot_nt(cot_ref[...], wd_ref[at, :])
        sig = jax.nn.sigmoid(gate)
        silu = gate * sig
        hid_ref[:, at] = (silu * up).astype(BF16)
        gg_ref[:, at] = (hgrad * up * sig * (1.0 + gate * (1.0 - sig))).astype(BF16)
        ug_ref[:, at] = (hgrad * silu).astype(BF16)
    ngrad_ref[...] = (dot_nt(gg_ref[...], wg_ref[...]) + dot_nt(ug_ref[...], wu_ref[...])).astype(BF16)
    out_ref[...] = dot_nn(hid_ref[...], wd_ref[...]).astype(BF16)


def mlp(ids, x, own, other, gains, wg, wu, wd, cots):
    full, hid = x.shape, (x.shape[0], wg.shape[1])
    outs = [(full, F32), (full, BF16), (hid, BF16), (hid, BF16), (hid, BF16), (full, BF16), (full, BF16)]
    return call(
        functools.partial(mlp_kernel, len(cots)), [(full, BF16)] + outs, "feed_forward",
        ids, x, own, other, gains, wg, wu, wd, anywhere=cots, scratch_shapes=[pltpu.SemaphoreType.DMA((2,))],
    )


def quarter(r, ids):
    core = 1 - ids[0] if r < 2 else ids[0]
    return 2 * core + (1 - ids[1] if r % 2 == 0 else ids[1])


def pieces_kernel(layouts, ids_ref, *refs):
    n = sum(len(layout) for _, layout in layouts)
    ins, outs = refs[: 2 * n], refs[2 * n :]
    i = 0
    for (base, layout), out_ref in zip(layouts, outs):
        for wide, begin, row, fold, lane in layout:
            a_ref, b_ref = ins[2 * i], ins[2 * i + 1]
            i += 1
            size = a_ref.shape[1] // 4
            for r in range(2):
                at = pl.multiple_of(quarter(base + r, ids_ref) * size, size)
                w = dot_tn(a_ref[:, pl.ds(at, size)], b_ref[:, begin : begin + wide]).astype(BF16)
                high = size // fold
                for f in range(fold):
                    lanes = slice(lane + f * wide, lane + (f + 1) * wide)
                    out_ref[r, row : row + high, lanes] = w[f * high : (f + 1) * high]


def pieces(ids, chunks, name):
    layouts = tuple((base, tuple(part[2:] for part in parts)) for base, parts, _, _ in chunks)
    args = [x for _, parts, _, _ in chunks for part in parts for x in part[:2]]
    outs = [((2, rows, width), BF16) for _, _, rows, width in chunks]
    return call(functools.partial(pieces_kernel, layouts), outs, name, ids, *args)


def place_kernel(layout, n, ids_ref, *refs):
    outs = refs[-len(layout) :]
    i = pl.program_id(0)

    def spread(piece):
        for out_ref, segments in zip(outs, layout):
            for row, high, fold, lane, wide, to in segments:
                h = high // fold
                for f in range(fold):
                    lanes = slice(lane + f * wide, lane + (f + 1) * wide)
                    out_ref[f * h : (f + 1) * h, to : to + wide] = piece[row : row + h, lanes].astype(F32)

    for k in range(n):
        pl.when(i == k)(functools.partial(lambda ref: spread(ref[...]), refs[k]))


def home(numbers, i, ids):
    r = sum(number * (i == k) for k, number in enumerate(numbers))
    core = jnp.where(r < 2, ids[0], 1 - ids[0])
    return 2 * core + jnp.where(r % 2 == 0, ids[1], 1 - ids[1])


def place(ids, numbers, sources, outs, name, earlier=None):
    earlier = earlier or [None] * len(outs)
    extra = [e for e in earlier if e is not None]
    n = len(sources)
    to = [k for k, e in enumerate(earlier) if e is not None]
    return pl.pallas_call(
        functools.partial(place_kernel, tuple(o[4] for o in outs), n),
        grid_spec=pltpu.PrefetchScalarGridSpec(
            num_scalar_prefetch=1,
            grid=(n,),
            in_specs=[pl.BlockSpec(memory_space=pltpu.VMEM)] * n + [pl.BlockSpec(memory_space=pl.ANY)] * len(extra),
            out_specs=[
                pl.BlockSpec((o[0], o[1]), functools.partial(lambda k, i, ids: (home(numbers, i, ids), k), o[2])) for o in outs
            ],
        ),
        out_shape=[jax.ShapeDtypeStruct((4 * o[0], o[3]), F32) for o in outs],
        input_output_aliases={1 + n + e: k for e, k in enumerate(to)},
        compiler_params=pltpu.CompilerParams(dimension_semantics=("arbitrary",), vmem_limit_bytes=24 * 1024 * 1024),
        name=name,
    )(ids, *(near(s) for s in sources), *extra)


def attn_bwd_kernel(heads, gains_ref, nother_ref, *refs):
    n = 14
    outs = refs[n : n + 7]
    bufs, (sem,) = refs[n + 7 : n + 7 + n], refs[n + 7 + n :]
    copies = [pltpu.make_async_copy(s, t, sem.at[i]) for i, (s, t) in enumerate(zip(refs[:n], bufs))]
    nown_ref, mid_ref, cot_ref, wo_ref, table_ref, v_ref, p_ref, krot_ref, qrot_ref, qraw_ref, kraw_ref = bufs[:11]
    wq_ref, wk_ref, wv_ref = bufs[11:]
    mgrad_ref, mgg_ref, blow_ref, qgrad_ref, kgrad_ref, vgrad_ref, n1g_ref = outs
    rows = kraw_ref.shape[0]
    groups = wk_ref.shape[1] // HEAD_SIZE
    q_gain, k_gain = gains_ref[2:3, :HEAD_SIZE], gains_ref[2:3, HEAD_SIZE : 2 * HEAD_SIZE]
    by_group = [
        [pltpu.make_async_copy(refs[6].at[g], p_ref.at[g], sem.at[n + 2 * g]),
         pltpu.make_async_copy(refs[8].at[g], qrot_ref.at[g], sem.at[n + 2 * g + 1])] for g in range(groups)
    ]
    for copy in copies[:4]:
        copy.start()
    for copy in copies[:3]:
        copy.wait()
    for copy in (copies[4], copies[5], copies[7], *by_group[0]):
        copy.start()
    ngrad = nown_ref[...].astype(F32) + nother_ref[...].astype(F32)
    middle = mid_ref[...]
    inv = inv_rms(middle)
    u = middle * inv
    mgg_ref[...] = jnp.sum(ngrad * u, 0, keepdims=True)
    s = ngrad * gains_ref[1:2, :]
    mgrad = cot_ref[...].astype(F32) + inv * (s - u * jnp.mean(s * u, -1, keepdims=True))
    mgrad_ref[...] = mgrad
    blow_ref[...] = mgrad.astype(BF16)
    for copy in (copies[9], copies[10], *(c for group in by_group[1:] for c in group), *copies[11:]):
        copy.start()
    scale = HEAD_SIZE ** (-0.5)
    copies[3].wait()
    copies[4].wait()
    cosine, sine = table_ref[:rows, :], table_ref[rows:, :]
    agrads = dot_nt(blow_ref[...], wo_ref[...]).astype(BF16)

    def back(raw, gain, grad):
        inv = inv_rms(raw)
        u = raw * inv
        dn = grad * cosine + pltpu.roll(grad * sine, HEAD_SIZE // 2, 1)
        s = dn * gain
        return (
            (inv * (s - u * jnp.mean(s * u, -1, keepdims=True))).astype(BF16),
            jnp.sum(dn * u, 0, keepdims=True),
        )

    qgg = jnp.zeros((1, HEAD_SIZE), F32)
    kgg = jnp.zeros((1, HEAD_SIZE), F32)
    for copy in (copies[5], copies[7]):
        copy.wait()
    for g in range(groups):
        for copy in (*by_group[g], *(copies[9:11] if g == 0 else ())):
            copy.wait()
        kv = slice(g * HEAD_SIZE, (g + 1) * HEAD_SIZE)
        krgrad, vgrad = 0.0, 0.0
        for h in range(heads):
            here = slice(h * rows, (h + 1) * rows)
            at = slice((g * heads + h) * HEAD_SIZE, (g * heads + h + 1) * HEAD_SIZE)
            agrad = agrads[:, at]
            prob = p_ref[g, here, :]
            prob_wide = prob.astype(F32)
            pgrad = dot_nt(agrad, v_ref[:, kv])
            sgrad = (prob_wide * (pgrad - jnp.sum(pgrad * prob_wide, -1, keepdims=True))).astype(BF16)
            vgrad += dot_tn(prob, agrad)
            krgrad += dot_tn(sgrad, qrot_ref[g, here, :])
            qgrad, part = back(qraw_ref[:, at].astype(F32), q_gain, dot_nn(sgrad, krot_ref[:, kv]) * scale)
            qgrad_ref[:, at] = qgrad
            qgg += part
        kgrad, part = back(kraw_ref[:, kv].astype(F32), k_gain, krgrad)
        kgrad_ref[:, kv] = kgrad
        vgrad_ref[:, kv] = vgrad.astype(BF16)
        kgg += part
    for copy in copies[11:]:
        copy.wait()
    total = (
        dot_nt(qgrad_ref[...], wq_ref[...]) + dot_nt(kgrad_ref[...], wk_ref[...]) + dot_nt(vgrad_ref[...], wv_ref[...])
    )
    width = total.shape[1]
    gains = jnp.concatenate([qgg, kgg, jnp.zeros((1, width - 2 * HEAD_SIZE), F32)], 1)
    gains = jnp.concatenate([gains, jnp.zeros((15, width), F32)], 0)
    n1g_ref[:rows] = total.astype(BF16)
    n1g_ref[rows:] = gains.astype(BF16)


def attn_bwd(nown, nother, middle, cot, gains, weights, prob, qraw, kraw, qrot, krot, v, tables):
    wq, wk, wv, wo = weights
    rows, width = middle.shape
    full = (rows, width)
    outs = [(full, F32), ((1, width), F32), (full, BF16), (qraw.shape, BF16), (kraw.shape, BF16), (kraw.shape, BF16),
            ((rows + 16, width), BF16)]
    streams = (nown, middle, cot, wo, tables, v, prob, krot, qrot, qraw, kraw, wq, wk, wv)
    return call(
        functools.partial(attn_bwd_kernel, wq.shape[1] // wk.shape[1]), outs, "attention_backward",
        gains, nother, anywhere=streams, megabytes=36,
        scratch_shapes=[pltpu.VMEM(a.shape, a.dtype) for a in streams] + [pltpu.SemaphoreType.DMA((len(streams) + 2 * prob.shape[0],))],
    )


def swap_pairs(n, bit):
    return [(i, i ^ bit) for i in range(n)]


def line_hops(n):
    step = n // 4
    shift = lambda a, b: [(a * step + r, b * step + r) for r in range(step)]
    return shift(0, 1) + shift(3, 2), shift(1, 2) + shift(2, 1), shift(1, 0) + shift(2, 3)


def add(a, b):
    return (a.astype(F32) + b.astype(F32)).astype(BF16)


def others(x, tensor):
    if tensor == 2:
        return lax.ppermute(x, "tensor", swap_pairs(2, 1))
    return (lax.psum(x.astype(F32), "tensor") - x.astype(F32)).astype(x.dtype)


def features(x, tensor):
    if tensor == 2:
        return x, lax.ppermute(x, "tensor", swap_pairs(2, 1))
    return (lax.all_gather(x, "tensor", axis=1, tiled=True),)


class Order:
    def __init__(self):
        self.last = None

    def __call__(self, step, *inputs):
        if self.last is not None:
            inputs, _ = lax.optimization_barrier((inputs, self.last))
        out = step(*inputs)
        self.last = jax.tree.leaves(out)
        return out


def per_device(
    dp, tensor, tokens, cotangent, attn_gain, query_weight, key_matrix, value_matrix, query_gain,
    key_norm_gain, out_weight, mlp_gain, gate_weight, up_weight, down_weight,
):
    rows, share = tokens.shape
    width = query_weight.shape[0]
    groups = key_matrix.shape[1] // HEAD_SIZE
    side = lax.axis_index("tensor")
    offset = side * share
    mine = lambda a: lax.dynamic_slice_in_dim(a, offset, share, 1)
    where = lax.axis_index("dp")
    core, pair, spot = where % 2, (where // 2) % 2, where // 4
    ids = jnp.stack([core, pair, side]).astype(jnp.int32)
    tables = jnp.asarray(np.concatenate(rope_tables(), 0))
    attn_gain = attn_gain[None]
    heads_gain = jnp.concatenate([query_gain, key_norm_gain, jnp.zeros((width - 2 * HEAD_SIZE,), F32)])[None]
    gains = jnp.concatenate([attn_gain, mlp_gain[None], heads_gain, jnp.zeros((5, width), F32)], 0)

    order = Order()
    xs = features(tokens, tensor)
    *xs, gains = order(lambda *a: a, *xs, order(lambda a: (a,), gains)[0])
    cots = features(order(lambda a: (a,), cotangent)[0], tensor)
    x, branch, n1, qraw, kraw, qrot, krot, v, prob, al = order(
        lambda *a: attn_fwd(ids, a, gains, query_weight, key_matrix, value_matrix, out_weight, tables), *xs)
    *cots, branch = order(lambda *a: a, *cots, branch)
    branch_got = others(branch, tensor)
    cot, middle, n2, hidden, ggrad, ugrad, mlp_part, ngrad = order(
        lambda own, other, *c: mlp(ids, x, own, other, gains, gate_weight, up_weight, down_weight, c),
        branch, branch_got, *cots)
    weights = (query_weight, key_matrix, value_matrix, out_weight)
    common = (gains, weights, prob, qraw, kraw, qrot, krot, v, tables)

    def ending(n1g, arrived, mgrad, mgg):
        n1_grad = n1g[:rows].astype(F32) + arrived[:rows].astype(F32)
        heads = n1g[rows : rows + 1].astype(F32) + arrived[rows : rows + 1].astype(F32)
        wide = x.astype(F32)
        inv_one = inv_rms(wide)
        u = wide * inv_one
        s = n1_grad * attn_gain
        mean = jnp.mean(s * u, -1, keepdims=True)
        input_grad = (mine(mgrad) + inv_one * (mine(s) - mine(u) * mean)).astype(BF16)
        return input_grad, jnp.concatenate([jnp.sum(n1_grad * u, 0, keepdims=True), mgg, heads], 0)

    if tensor != 2 or dp != 16:
        mgrad, mgg, blow, qgrad, kgrad, vgrad, n1g = attn_bwd(
            ngrad, others(ngrad, tensor), middle, cot, *common)
        input_grad, gains = ending(n1g, others(n1g, tensor), mgrad, mgg)
        total = lambda a: lax.psum(a.astype(BF16), "dp").astype(F32)
        agg, mgg, heads = total(lax.pmean(gains, "tensor"))
        layer_out = (mine(middle) + lax.psum_scatter(mlp_part, "tensor", scatter_dimension=1, tiled=True)).astype(BF16)
        return (
            layer_out, input_grad, agg, total(dot_tn(n1, qgrad)), total(dot_tn(n1, kgrad)), total(dot_tn(n1, vgrad)),
            heads[:HEAD_SIZE], heads[HEAD_SIZE : 2 * HEAD_SIZE], total(dot_tn(al, blow)), mgg,
            total(dot_tn(n2, ggrad)), total(dot_tn(n2, ugrad)), total(dot_tn(hidden, cot)),
        )

    edge = (spot == 0) | (spot == 3)
    inward, across, outward = line_hops(dp)
    between = inward + outward
    send = lambda x, hops: lax.ppermute(x, "dp", hops)
    over_core = lambda x: send(x, swap_pairs(dp, 1))
    over_pair = lambda x: send(x, swap_pairs(dp, 2))
    over_tensor = lambda x: lax.ppermute(x, "tensor", swap_pairs(2, 1))
    half = lambda a, b: lax.dynamic_slice_in_dim(a, b * share, share, 1)
    first = lambda keep, got: (add(keep[0], got[0]), add(keep[1], got[1]))
    same = lambda *a: a

    units, wide = gate_weight.shape[1], qraw.shape[1]
    high, low, thin = width // 4, width // 8, wide // 2
    size = hidden.shape[1] // 4
    rest = units - width

    def hidden_parts(a, b):
        return [(a, b, width, 0, 0, 1, 0), (a, b, rest, width, high, 2, 0)]

    hidden_outs = [(high, units, 0, units, ((0, high, 1, 0, width, 0), (high, high, 2, 0, rest, width)))]
    down_outs = [(size, width, 0, width, ((0, size, 1, 0, width, 0),))]

    nother = over_tensor(ngrad)
    send_d, keep_d = order(lambda h, c: pieces(ids, [(base, [(h, c, width, 0, 0, 1, 0)], size, width) for base in (0, 2)],
                                               "down_gradient"), hidden, cot)
    got_d = over_core(send_d)
    send_g, send_u = order(
        lambda n2, g, u: pieces(ids, [(0, hidden_parts(n2, g), size, width), (0, hidden_parts(n2, u), size, width)],
                                "gate_up_gradient_sent"), n2, ggrad, ugrad)
    x_d, d = order(first, keep_d, got_d)
    pair_d = over_pair(x_d)
    got_g, got_u = over_core(send_g), over_core(send_u)
    keep_g, keep_u = order(
        lambda n2, g, u: pieces(ids, [(2, hidden_parts(n2, g), size, width), (2, hidden_parts(n2, u), size, width)],
                                "gate_up_gradient_kept"), n2, ggrad, ugrad)
    x_g, g, x_u, u = order(lambda a, b, c, d: (*first(a, b), *first(c, d)), keep_g, got_g, keep_u, got_u)
    pair_d, nother, x_g = order(same, pair_d, nother, x_g)
    pair_g = over_pair(x_g)
    d, mlp_half = order(lambda a, b, m: (add(a, b), half(m, 1 - side)), d, pair_d, mlp_part)
    line_d, mlp_got = send(d, inward), over_tensor(mlp_half)
    mgrad, mgg, blow, qgrad, kgrad, vgrad, n1g = order(
        lambda *a: attn_bwd(*a, *common), ngrad, nother, middle, cot)

    def out_pieces(al, blow, n1, qgrad):
        parts = [(al, blow, width, 0, 0, 1, 0), (n1, qgrad, thin, 0, high, 2, 0)]
        return pieces(ids, [(base, parts, high + low, width) for base in (0, 2)], "out_query_gradient")

    def kv_pieces(n1, qgrad, kgrad, vgrad):
        parts = [(n1, kgrad, thin, 0, 0, 1, 0), (n1, vgrad, thin, 0, 0, 1, thin), (n1, qgrad, thin, thin, high, 2, 0)]
        return pieces(ids, [(base, parts, high + low, width) for base in (0, 2)], "key_value_query_gradient")

    send_o, keep_o = order(out_pieces, al, blow, n1, qgrad)
    line_d, pair_g, x_u, send_o = order(same, line_d, pair_g, x_u, send_o)
    pair_u = over_pair(x_u)
    got_o = over_core(send_o)
    d, g = order(lambda d, line, g, pair: (add(d, line), add(g, pair)), d, line_d, g, pair_g)
    mid_d, line_g = send(d, across), send(g, inward)
    send_k, keep_k = order(kv_pieces, n1, qgrad, kgrad, vgrad)
    x_o, o = order(first, keep_o, got_o)
    pair_u, x_o, send_k = order(same, pair_u, x_o, send_k)
    pair_o = over_pair(x_o)
    got_k = over_core(send_k)

    def layer(middle, part, got):
        return (mine(middle) + (mine(part).astype(F32) + got.astype(F32))).astype(BF16)

    layer_out = order(layer, middle, mlp_part, mlp_got)

    def turn(kept, line, inner, mid, new, pair):
        inner = add(inner, mid)
        new = add(new, pair)
        return jnp.where(edge, new, inner), add(kept, line), inner, new

    step, g, d, u = order(turn, g, line_g, d, mid_d, u, pair_u)
    line_du, mid_g = send(step, between), send(g, across)
    arrived = over_tensor(n1g)
    x_k, k = order(first, keep_k, got_k)
    pair_o, x_k = order(same, pair_o, x_k)
    pair_k = over_pair(x_k)

    def z(out, line, new, inner, mid, newest, pair):
        inner = add(inner, mid)
        newest = add(newest, pair)
        return jnp.where(edge, newest, inner), add(new, line), jnp.where(edge, line, out), inner, newest

    step, u, d, g, o = order(z, d, line_du, u, g, mid_g, o, pair_o)
    line_go, mid_u = send(step, between), send(u, across)
    pair_k, d = order(same, pair_k, d)
    near_d = over_pair(d)
    input_grad, gains = order(ending, n1g, arrived, mgrad, mgg)

    def z_last(out, line, new, inner, mid, newest, pair, gains):
        inner = add(inner, mid)
        newest = jnp.concatenate([add(newest, pair), jnp.pad(gains, ((0, 13), (0, 0))).astype(BF16)], 0)
        step = jnp.where(edge, newest, jnp.pad(inner, ((0, 16), (0, 0))))
        return step, add(new, line), jnp.where(edge, line, out), inner, newest

    step, o, g, u, k = order(z_last, g, line_go, o, u, mid_u, k, pair_k, gains)
    line_uk, mid_o = send(step, between), send(o, across)
    near_d, g = order(same, near_d, g)
    near_g = over_pair(g)
    far_d, far_near_d = over_core(d), over_core(near_d)
    u, k, o = order(lambda u, line, k, o, mid: (jnp.where(edge, line[: high + low], u), add(k, line), add(o, mid)),
                    u, line_uk, k, o, mid_o)
    line_o, mid_k = send(o, outward), send(k, across)
    near_g, u = order(same, near_g, u)
    near_u = over_pair(u)
    far_g, far_near_g = over_core(g), over_core(near_g)
    (down_wgrad,) = order(lambda *a: place(ids, (0, 1, 2, 3), a, down_outs, "down_place"), d, near_d, far_d, far_near_d)
    o, k = order(lambda o, line, k, mid: (jnp.where(edge, line, o), add(k, mid)), o, line_o, k, mid_k)
    line_k = send(k, outward)
    near_u, o = order(same, near_u, o)
    near_o = over_pair(o)
    far_u, far_near_u = over_core(u), over_core(near_u)
    (gate_wgrad,) = order(lambda *a: place(ids, (0, 1, 2, 3), a, hidden_outs, "gate_place"), g, near_g, far_g, far_near_g)
    k = order(lambda k, line: jnp.where(edge, line, k), k, line_k)
    near_o, k = order(same, near_o, k)
    near_k = over_pair(k)
    far_o, far_near_o, far_k = over_core(o), over_core(near_o), over_core(k)
    (up_wgrad,) = order(lambda *a: place(ids, (0, 1, 2, 3), a, hidden_outs, "up_place"), u, near_u, far_u, far_near_u)
    out_wgrad, query_wgrad = order(
        lambda *a: place(
            ids, (0, 1, 2, 3), a, [(high, width, 0, width, ((0, high, 1, 0, width, 0),)),
                        (high, thin, 0, wide, ((high, high, 2, 0, thin, 0),))], "out_query_place"),
        o, near_o, far_o, far_near_o)
    last_outs = [
        (high, thin, 0, thin, ((0, high, 1, 0, thin, 0),)), (high, thin, 0, thin, ((0, high, 1, thin, thin, 0),)),
        (high, thin, 1, wide, ((high, high, 2, 0, thin, 0),)), (16, width, 0, width, ((high + low, 16, 1, 0, width, 0),))]
    key_wgrad, value_wgrad, query_wgrad, gains = order(
        lambda k, far, q: place(ids, (0, 2), [k, far], last_outs, "own_place", [None, None, q, None]), k, far_k,
        query_wgrad)
    (near_k,) = order(lambda a: (a,), near_k)
    far_near_k = over_core(near_k)
    key_wgrad, value_wgrad, query_wgrad, gains = order(
        lambda a, *e: place(ids, (1,), [a], last_outs, "beside_place", e), near_k, key_wgrad, value_wgrad,
        query_wgrad, gains)
    key_wgrad, value_wgrad, query_wgrad, gains = order(
        lambda a, *e: place(ids, (3,), [a], last_outs, "far_place", e), far_near_k, key_wgrad, value_wgrad, query_wgrad, gains)
    gains = gains.reshape(4, 16, width).sum(0)
    return (
        layer_out, input_grad, gains[0], query_wgrad, key_wgrad, value_wgrad,
        gains[2, :HEAD_SIZE], gains[2, HEAD_SIZE : 2 * HEAD_SIZE], out_wgrad,
        gains[1], gate_wgrad, up_wgrad, down_wgrad,
    )


def solution(mesh):
    rows, cols, rep = P("tensor", None), P(None, "tensor"), P()
    both = P("dp", "tensor")
    return jax.shard_map(
        functools.partial(per_device, mesh.shape["dp"], mesh.shape["tensor"]),
        mesh=mesh,
        in_specs=(both, both, rep, cols, cols, cols, rep, rep, rows, rep, cols, cols, rows),
        out_specs=(both, both, rep, cols, cols, cols, rep, rep, rows, rep, cols, cols, rows),
        check_vma=False,
    )
```
